512 devices in a mesh: ctx: 64 (over y_hi, z, core), ch: 8 (over y_lo, x).
Axes of the slice: x: 4, y: 8 (y_hi: 4, y_lo: 2; y = y_hi * 2 + y_lo), z: 8, core: 2. Of those that a mesh axis runs over, the one named last changes fastest.
Arguments:
- inputs: bfloat16 [16384, 4096], P('ctx', 'ch'), may hold values from -6 to 6
- out_grad: bfloat16 [16384, 4096], P('ctx', 'ch'), may hold values from -6 to 6
- decay_rate: float32 [16, 512], replicated, may hold values from 1.5258789e-05 to 0.05, as said below
- residue: float32 [16, 512], replicated, may hold values from -1.5 to 1.5
- skip_gain: float32 [4096], P('ch'), may hold values from -6 to 6
Outputs:
- input_grad: float32 [16384, 4096], P('ctx', 'ch')
- filter_grad: float32 [16384, 512], P('ctx', 'ch')
The draws below stay inside these ranges and needn't reach their ends.
Inputs may be any that keep to these rules, and one draw needn't show every extreme that they name: `decay_rate`: each decay rate lies either between 0.3 / 16384 and 2 / 16384 or between 1 / 50 and 1 / 25.
All inputs are finite; a program needn't handle non-finite values.
Results may differ from the reference program's by a relative error of at most 0.00055.
Values may be sent and summed in bfloat16 or wider, within the bound.
A program may use at most 64 MiB of HBM per device.

```python
import math
import jax
import jax.numpy as jnp
from jax import lax

FILTERS = 512
MODES = 16
SEQ = 16384
CH = 4096
SHARE = 8


def draw_decay_rate(key, part):
    key = jax.random.fold_in(key, 7)
    first, second, third = jax.random.split(key, 3)
    shape = (MODES, FILTERS)
    slow_share = 0.5
    picked = jax.random.uniform(first, shape, jnp.float32) < slow_share
    slow = jnp.exp(jax.random.uniform(second, shape, jnp.float32, math.log(0.3), math.log(2.0))) / SEQ
    fast = jnp.exp(jax.random.uniform(third, shape, jnp.float32, math.log(1.0 / 50.0), math.log(1.0 / 25.0)))
    return jnp.where(picked, slow, fast).astype(jnp.float32)


def levels(key, extent, shards, least, largest):
    level = 1.0
    for position, blocks in shards:
        heights = jax.random.uniform(jax.random.fold_in(jax.random.fold_in(key, 6), position), (blocks,), jnp.float32, least / len(shards), largest / len(shards))
        level = level * jnp.repeat(jnp.exp(heights), extent[position] // blocks).reshape((-1,) + (1,) * (len(extent) - 1 - position))
    return level


def scatter_about(own_key, shape, deviation, bound, shards=(), kind=jnp.bfloat16):
    values = jax.random.normal(own_key, shape, jnp.float32) * deviation
    if len(shards) > 0:
        values = levels(own_key, shape, shards, -0.22, 0.18) * values
    return jnp.clip(values, min=-bound, max=bound).astype(kind)


def setup_inputs(seed: int = 0) -> dict:
    key_of = jax.random.split(jax.random.key(seed), 6)
    return {
        "inputs": scatter_about(key_of[0], (SEQ, CH), 1.0, 6.0, ((0, 64), (1, 8))),
        "out_grad": scatter_about(key_of[1], (SEQ, CH), 1.0, 6.0, ((0, 64), (1, 8))),
        "decay_rate": draw_decay_rate(jax.random.fold_in(key_of[5], 71), 0),
        "residue": scatter_about(key_of[3], (MODES, FILTERS), 0.25, 1.5, (), jnp.float32),
        "skip_gain": scatter_about(key_of[4], (CH,), 1.0, 6.0, ((0, 8),), jnp.float32),
    }


def build_filter(decay_rate, residue, positions):
    filters = jnp.zeros((positions.shape[0], decay_rate.shape[1]), jnp.float32)
    for mode in range(MODES):
        rate = decay_rate[mode][None, :]
        weight = residue[mode][None, :] * jnp.sqrt(-jnp.expm1(-2.0 * rate))
        filters = filters + weight * jnp.exp(-rate * positions[:, None])
    return filters

def reference(inputs, out_grad, decay_rate, residue, skip_gain):
    full_len = 2 * SEQ
    positions = jnp.arange(SEQ).astype(jnp.float32)
    filters = build_filter(decay_rate, residue, positions)
    filter_spec = jnp.fft.fft(filters, n=full_len, axis=0)
    grouped_in = inputs.astype(jnp.float32).reshape(SEQ, SHARE, FILTERS).transpose(1, 0, 2)
    grouped_grad = out_grad.astype(jnp.float32).reshape(SEQ, SHARE, FILTERS).transpose(1, 0, 2)
    gains = skip_gain.reshape(SHARE, FILTERS)

    def one_group(running, members):
        signal, gradient, gain_row = members
        signal_spec = jnp.fft.fft(signal, n=full_len, axis=0)
        grad_spec = jnp.fft.fft(gradient, n=full_len, axis=0)
        input_term = jnp.conj(filter_spec) * grad_spec
        result = jnp.real(jnp.fft.ifft(input_term, axis=0))[:SEQ] + gain_row[None, :] * gradient
        return (running + jnp.conj(signal_spec) * grad_spec, result.astype(jnp.float32))
    initial = 0.0 * filter_spec
    filter_sum, results = lax.scan(one_group, initial, (grouped_in, grouped_grad, gains))
    input_grad = results.transpose(1, 0, 2).reshape(SEQ, SHARE * FILTERS)
    filter_grad = jnp.real(jnp.fft.ifft(filter_sum, axis=0))[:SEQ] / math.sqrt(SEQ * SHARE)
    return (input_grad, filter_grad.astype(jnp.float32))
```

```python
import functools
import math

import jax
import jax.numpy as jnp
import ml_dtypes
import numpy as np
from jax import lax
from jax.experimental import pallas as pl
from jax.experimental.pallas import tpu as pltpu
from jax.sharding import PartitionSpec as P

MESH = pl.DeviceIdType.MESH
F32 = jnp.float32
BF16 = jnp.bfloat16


def halves(table):
    high = table.astype(np.float32).astype(ml_dtypes.bfloat16)
    low = (table - high.astype(np.float64)).astype(np.float32).astype(ml_dtypes.bfloat16)
    return high, low


@functools.lru_cache(maxsize=None)
def tables(nc, nh, sd):
    rows = 2 * nh
    j = np.arange(nc) + 0.5
    a = np.arange(nc)
    s = np.arange(sd)
    full = 2 * nc * sd
    angle = 2.0 * np.pi * np.outer(j, a) / (2 * nc)
    block = np.concatenate([np.cos(angle), -np.sin(angle)], axis=0)
    high, low = halves(block)
    first = np.concatenate([high, low], axis=1)
    last_h, last_l = halves(block.T.copy())
    last = np.concatenate([last_h, last_h, last_l], axis=1)
    angle = 2.0 * np.pi * np.outer(j, s) / full
    twist = np.stack([np.cos(angle), np.sin(angle)]).astype(np.float32)
    angle = 2.0 * np.pi * (np.outer(s, s) % sd) / sd
    cos, sin = np.cos(angle), np.sin(angle)
    step = np.concatenate([np.concatenate([cos, -sin], axis=1), np.concatenate([sin, cos], axis=1)], axis=0)
    high, low = halves(step)
    second = np.concatenate([high, high, low], axis=0)
    angle = 2.0 * np.pi * np.outer(s + 0.5, s) / (2 * sd)
    near = np.concatenate([np.cos(angle), -np.sin(angle)], axis=0)
    high, low = halves(near)
    near_in = np.concatenate([high, low, high], axis=1)
    near_out = np.concatenate([high.T, high.T, low.T], axis=1)
    size = 16 * rows
    perm = np.zeros((size, size), np.float32)
    for f in range(16):
        for r in range(rows):
            perm[f * rows + r, r * 16 + f] = 1.0
    bf = ml_dtypes.bfloat16
    return (
        perm.astype(bf),
        perm.T.copy().astype(bf),
        first,
        np.ascontiguousarray(second),
        last,
        twist,
        near_in,
        np.ascontiguousarray(near_out),
    )


def split(value):
    high = value.astype(BF16)
    return high, (value - high.astype(F32)).astype(BF16)


def dot(left, right):
    return jnp.dot(left, right, preferred_element_type=F32)


def kernel(nc, nh, modes, *refs):
    (x_ref, g_ref, rate_ref, res_ref, gain_ref), refs = refs[:5], refs[5:]
    table_in, refs = refs[:8], refs[8:]
    (y_ref, out_ref), refs = refs[:2], refs[2:]
    (perm, perm_t, first, second, last, twist, near_in, near_out), refs = refs[:8], refs[8:]
    (s1, r1, s2, r2, u_own, u_all, st_own, st_all, t_own, t_all), refs = refs[:10], refs[10:]
    (grad, taps, eb, ww, rate_rows, blocks, left, spec), refs = refs[:8], refs[8:]
    (table_sem, send1, recv1, send2, recv2, send_u, recv_u, send_s, recv_s, send_t, recv_t) = refs

    sd, cols = x_ref.shape
    rows = 2 * nh
    cb = modes * cols // nc
    nblk = cols // cb
    tiles = sd // 8
    me = lax.axis_index("ctx")
    my = lax.axis_index("ch")

    def ctx_peer(k):
        return lax.rem(me + k, nc)

    def ch_peer(k):
        return lax.rem(my + k, nh)

    barrier = pltpu.get_barrier_semaphore()

    def greet_ch(k, _):
        pl.semaphore_signal(barrier, inc=1, device_id={"ch": ch_peer(k)}, device_id_type=MESH)
        return 0

    def greet_ctx(k, _):
        pl.semaphore_signal(barrier, inc=1, device_id={"ctx": ctx_peer(k)}, device_id_type=MESH)
        return 0

    lax.fori_loop(1, nh, greet_ch, 0)
    lax.fori_loop(1, nc, greet_ctx, 0)

    loads = [
        pltpu.make_async_copy(src, dst, table_sem.at[n])
        for n, (src, dst) in enumerate(
            zip(table_in, (perm, perm_t, first, second, last, twist, near_in, near_out))
        )
    ]
    for load in loads:
        load.start()

    width = min(cols, 256)
    eye = (
        lax.broadcasted_iota(jnp.int32, (width, width), 0)
        == lax.broadcasted_iota(jnp.int32, (width, width), 1)
    ).astype(F32).astype(BF16)
    for arr, ref in enumerate((x_ref, g_ref)):
        for c0 in range(0, cols, width):
            turned = lax.dot_general(
                eye, ref[:, c0 : c0 + width], (((1,), (1,)), ((), ())), preferred_element_type=F32
            ).astype(BF16)
            turned = turned.reshape(width // nc, nc, sd)
            for k in range(width // nc):
                s1[c0 // nc + k, arr] = turned[k]

    pl.semaphore_wait(barrier, nh - 1 + nc - 1)

    def copy1(k, src, dst):
        return pltpu.make_async_remote_copy(
            src_ref=src, dst_ref=dst, send_sem=send1, recv_sem=recv1, device_id={"ch": ch_peer(k)}, device_id_type=MESH
        )

    def send_ch(k, _):
        copy1(k, s1.at[ch_peer(k)], r1.at[my]).start()
        return 0

    lax.fori_loop(1, nh, send_ch, 0)
    r1[pl.ds(my, 1)] = s1[pl.ds(my, 1)]

    grad[...] = g_ref[...].astype(F32)
    eight = lax.broadcasted_iota(jnp.int32, (8, cb), 0).astype(F32)
    octs = 8.0 * lax.broadcasted_iota(jnp.int32, (tiles, cb), 0).astype(F32)

    def weight_of(rate, residue):
        x = 2.0 * rate
        series = 1.0 - x * (1.0 / 7.0)
        for n in (6, 5, 4, 3, 2):
            series = 1.0 - (x * (1.0 / n)) * series
        return residue * jnp.sqrt(x * series)

    def columns(blk):
        return pl.ds(pl.multiple_of(blk * cb, cb), cb)

    def states(blk, _):
        at = columns(blk)
        rate = rate_ref[:, at]
        weight = weight_of(rate, res_ref[:, at])
        ww[:, at] = weight
        for n in range(modes):
            slow = jnp.exp(-rate[n : n + 1] * octs)
            eb[n] = slow
        fine = [jnp.exp(-rate[n : n + 1] * eight) for n in range(modes)]
        scaled = [fine[n] * weight[n : n + 1] for n in range(modes)]
        sums = [jnp.zeros((8, cb), F32) for _ in range(modes)]
        for t in range(tiles):
            g = grad[8 * t : 8 * t + 8, at]
            tap = jnp.zeros((8, cb), F32)
            for n in range(modes):
                level = jnp.broadcast_to(eb[n, t : t + 1], (8, cb))
                sums[n] = sums[n] + level * g
                tap = tap + level * scaled[n]
            taps[8 * t : 8 * t + 8, at] = tap
        for n in range(modes):
            rate_rows[n * nblk + blk] = rate[n : n + 1]
            u_own[n * nblk + blk] = jnp.sum(sums[n] * fine[n], axis=0, keepdims=True)
        return 0

    lax.fori_loop(0, nblk, states, 0)

    def ctx_copy(k, src, dst, send, recv):
        return pltpu.make_async_remote_copy(
            src_ref=src, dst_ref=dst, send_sem=send, recv_sem=recv, device_id={"ctx": ctx_peer(k)}, device_id_type=MESH
        )

    def send_to_ctx(own, everyone, send, recv):
        def body(k, _):
            ctx_copy(k, own.at[ctx_peer(k)], everyone.at[me], send, recv).start()
            return 0

        lax.fori_loop(1, nc, body, 0)
        everyone[pl.ds(me, 1)] = own[pl.ds(me, 1)]

    def wait_ctx(own, everyone, send, recv):
        return ctx_copy(1, own.at[pl.ds(0, nc - 1)], everyone.at[pl.ds(0, nc - 1)], send, recv)

    send_to_ctx(u_own, u_all, send_u, recv_u)

    whole1 = copy1(1, s1.at[pl.ds(0, nh - 1)], r1.at[pl.ds(0, nh - 1)])
    whole1.wait_recv()
    loads[0].wait()
    loads[1].wait()
    for f0 in range(0, nc, 16):
        block = r1[:, :, f0 : f0 + 16, :].reshape(rows * 16, sd)
        s2[f0 : f0 + 16] = dot(perm[...], block).astype(BF16).reshape(16, rows, sd)
    send_to_ctx(s2, r2, send2, recv2)

    wait_ctx(u_own, u_all, send_u, recv_u).wait_recv()
    decay = jnp.exp(-rate_rows[me] * float(sd))
    state = jnp.zeros((1, cb), F32)
    for p in range(nc - 1, -1, -1):
        st_own[p] = state
        state = u_all[p] + decay * state
    send_to_ctx(st_own, st_all, send_s, recv_s)

    loads[6].wait()
    loads[7].wait()
    wide = min(cols, 256)

    def inside(blk, _):
        at = pl.ds(pl.multiple_of(blk * wide, wide), wide)
        g = g_ref[:, at]
        g_spec = dot(near_in[:, : 2 * sd], jnp.concatenate([g, g], axis=0))
        high, low = split(taps[:, at])
        h_spec = dot(near_in[...], jnp.concatenate([high, high, low], axis=0))
        g_re, g_im = g_spec[:sd], g_spec[sd:]
        h_re, h_im = h_spec[:sd], h_spec[sd:]
        term = jnp.concatenate([h_re * g_re + h_im * g_im, h_re * g_im - h_im * g_re], axis=0)
        high, low = split(term)
        near = dot(near_out[...], jnp.concatenate([high, low, high], axis=0)) * (1.0 / sd)
        y_ref[:, at] = near + gain_ref[:, at] * grad[:, at]
        return 0

    lax.fori_loop(0, cols // wide, inside, 0)

    wait_ctx(st_own, st_all, send_s, recv_s).wait_recv()

    def outside(blk, _):
        at = columns(blk)
        rate = rate_ref[:, at]
        weight = ww[:, at]
        fine = []
        for n in range(modes):
            carried = weight[n : n + 1] * st_all[n * nblk + blk]
            eb[n] = carried * jnp.exp(-rate[n : n + 1] * (float(sd - 8) - octs))
            fine.append(jnp.exp(-rate[n : n + 1] * (8.0 - eight)))
        for t in range(tiles):
            total = y_ref[8 * t : 8 * t + 8, at]
            for n in range(modes):
                total = total + jnp.broadcast_to(eb[n, t : t + 1], (8, cb)) * fine[n]
            y_ref[8 * t : 8 * t + 8, at] = total
        return 0

    lax.fori_loop(0, nblk, outside, 0)

    for n in (2, 3, 4, 5):
        loads[n].wait()
    wait_ctx(s2, r2, send2, recv2).wait_recv()
    for a0 in range(0, nc, 16):
        block = r2[a0 : a0 + 16].reshape(16 * rows, sd)
        blocks[:, a0 : a0 + 16, :] = dot(perm_t[...], block).astype(BF16).reshape(rows, 16, sd)
    turn_c, turn_s = twist[0], twist[1]
    spec[...] = jnp.zeros_like(spec)

    def pair(q, _):
        for k in range(4):
            part = blocks[4 * q + k]
            freq = dot(first[...], jnp.concatenate([part, part], axis=0))
            re, im = freq[:nc], freq[nc:]
            high_re, low_re = split(re * turn_c + im * turn_s)
            high_im, low_im = split(im * turn_c - re * turn_s)
            at = pl.ds(((k % 2) * 2 + k // 2) * nc, nc)
            for n, piece in enumerate((high_re, high_im, low_re, low_im, high_re, high_im)):
                left[at, n * sd : (n + 1) * sd] = piece
        both = dot(left[...], second[...])
        x_re, x_im = both[: 2 * nc, :sd], both[: 2 * nc, sd:]
        g_re, g_im = both[2 * nc :, :sd], both[2 * nc :, sd:]
        re = x_re * g_re + x_im * g_im
        im = x_re * g_im - x_im * g_re
        spec[:, :sd] += re[:nc] + re[nc:]
        spec[:, sd:] += im[:nc] + im[nc:]
        return 0

    lax.fori_loop(0, nh // 2, pair, 0)

    re_h, re_l = split(spec[:, :sd])
    im_h, im_l = split(-spec[:, sd:])
    both = dot(jnp.concatenate([re_h, im_h, re_l, im_l, re_h, im_h], axis=1), second[...])
    re, im = both[:, :sd], -both[:, sd:]
    high, low = split(
        jnp.concatenate([re * turn_c - im * turn_s, im * turn_c + re * turn_s], axis=0)
    )
    scale = 2.0 / (2 * nc * sd) / math.sqrt(nc * sd * nh)
    result = dot(last[...], jnp.concatenate([high, low, high], axis=0)) * scale
    for d in range(nc):
        t_own[d] = result[d : d + 1]
    send_to_ctx(t_own, t_all, send_t, recv_t)
    wait_ctx(t_own, t_all, send_t, recv_t).wait_recv()
    gathered = jnp.concatenate([t_all[d] for d in range(nc)], axis=0)
    out_ref[...] = gathered.T

    whole1.wait_send()
    wait_ctx(s2, r2, send2, recv2).wait_send()
    wait_ctx(u_own, u_all, send_u, recv_u).wait_send()
    wait_ctx(st_own, st_all, send_s, recv_s).wait_send()
    wait_ctx(t_own, t_all, send_t, recv_t).wait_send()


def body(nc, nh, inputs, out_grad, decay_rate, residue, skip_gain):
    sd, cols = inputs.shape
    modes = decay_rate.shape[0]
    rows = 2 * nh
    cb = modes * cols // nc
    consts = [jnp.asarray(t) for t in tables(nc, nh, sd)]
    vmem = pl.BlockSpec(memory_space=pltpu.VMEM)
    dma = pltpu.SemaphoreType.DMA
    return pl.pallas_call(
        functools.partial(kernel, nc, nh, modes),
        out_shape=(
            jax.ShapeDtypeStruct((sd, cols), F32),
            jax.ShapeDtypeStruct((sd, nc), F32),
        ),
        in_specs=[vmem] * 5 + [pl.BlockSpec(memory_space=pl.ANY)] * len(consts),
        out_specs=(vmem, vmem),
        scratch_shapes=[pltpu.VMEM(c.shape, c.dtype) for c in consts]
        + [
            pltpu.VMEM((nh, 2, nc, sd), BF16),
            pltpu.VMEM((nh, 2, nc, sd), BF16),
            pltpu.VMEM((nc, rows, sd), BF16),
            pltpu.VMEM((nc, rows, sd), BF16),
            pltpu.VMEM((nc, 1, cb), F32),
            pltpu.VMEM((nc, 1, cb), F32),
            pltpu.VMEM((nc, 1, cb), F32),
            pltpu.VMEM((nc, 1, cb), F32),
            pltpu.VMEM((nc, 1, sd), F32),
            pltpu.VMEM((nc, 1, sd), F32),
            pltpu.VMEM((sd, cols), F32),
            pltpu.VMEM((sd, cols), F32),
            pltpu.VMEM((modes, sd // 8, cb), F32),
            pltpu.VMEM((modes, cols), F32),
            pltpu.VMEM((nc, 1, cb), F32),
            pltpu.VMEM((rows, nc, sd), BF16),
            pltpu.VMEM((4 * nc, 6 * sd), BF16),
            pltpu.VMEM((nc, 2 * sd), F32),
            dma((len(consts),)),
        ]
        + [dma] * 10,
        compiler_params=pltpu.CompilerParams(
            collective_id=0, has_side_effects=True, vmem_limit_bytes=48 * 1024 * 1024
        ),
        name="modal_backward",
    )(inputs, out_grad, decay_rate, residue, skip_gain.reshape(1, cols), *consts)


def solution(mesh):
    placed = (P("ctx", "ch"), P("ctx", "ch"), P(), P(), P("ch"))
    return jax.shard_map(
        functools.partial(body, mesh.shape["ctx"], mesh.shape["ch"]),
        mesh=mesh,
        in_specs=placed,
        out_specs=(P("ctx", "ch"), P("ctx", "ch")),
        check_vma=False,
    )
```

```python
import functools
import math

import jax
import jax.numpy as jnp
import ml_dtypes
import numpy as np
from jax import lax
from jax.experimental import pallas as pl
from jax.experimental.pallas import tpu as pltpu
from jax.sharding import PartitionSpec as P

MESH = pl.DeviceIdType.MESH
F32 = jnp.float32
BF16 = jnp.bfloat16


def halves(table):
    high = table.astype(np.float32).astype(ml_dtypes.bfloat16)
    low = (table - high.astype(np.float64)).astype(np.float32).astype(ml_dtypes.bfloat16)
    return high, low


@functools.lru_cache(maxsize=None)
def tables(nc, nh, sd):
    rows = 2 * nh
    j = np.arange(nc) + 0.5
    a = np.arange(nc)
    s = np.arange(sd)
    full = 2 * nc * sd
    angle = 2.0 * np.pi * np.outer(j, a) / (2 * nc)
    block = np.concatenate([np.cos(angle), -np.sin(angle)], axis=0)
    high, low = halves(block)
    first = np.concatenate([high, low], axis=1)
    last_h, last_l = halves(block.T.copy())
    last = np.concatenate([last_h, last_h, last_l], axis=1)
    angle = 2.0 * np.pi * np.outer(j, s) / full
    twist = np.stack([np.cos(angle), np.sin(angle)]).astype(np.float32)
    angle = 2.0 * np.pi * (np.outer(s, s) % sd) / sd
    cos, sin = np.cos(angle), np.sin(angle)
    step = np.concatenate([np.concatenate([cos, -sin], axis=1), np.concatenate([sin, cos], axis=1)], axis=0)
    high, low = halves(step)
    second = np.concatenate([high, high, low], axis=0)
    angle = 2.0 * np.pi * np.outer(s + 0.5, s) / (2 * sd)
    near = np.concatenate([np.cos(angle), -np.sin(angle)], axis=0)
    high, low = halves(near)
    near_in = np.concatenate([high, low, high], axis=1)
    near_out = np.concatenate([high.T, high.T, low.T], axis=1)
    size = 16 * rows
    perm = np.zeros((size, size), np.float32)
    for f in range(16):
        for r in range(rows):
            perm[f * rows + r, r * 16 + f] = 1.0
    bf = ml_dtypes.bfloat16
    return (
        perm.astype(bf),
        perm.T.copy().astype(bf),
        first,
        np.ascontiguousarray(second),
        last,
        twist,
        near_in,
        np.ascontiguousarray(near_out),
    )


def split(value):
    high = value.astype(BF16)
    return high, (value - high.astype(F32)).astype(BF16)


def dot(left, right):
    return jnp.dot(left, right, preferred_element_type=F32)


def kernel(nc, nh, modes, *refs):
    args_in, refs = refs[:13], refs[13:]
    (y_ref, out_ref), refs = refs[:2], refs[2:]
    args, refs = refs[:13], refs[13:]
    x_ref, g_ref, rate_ref, res_ref, gain_ref, perm, perm_t, first, second, last, twist, near_in, near_out = args
    (s1, r1, s2, r2, u_own, u_all, st_own, st_all, t_own, t_all), refs = refs[:10], refs[10:]
    (y, grad, taps, eb, ww, rate_rows, blocks, left, spec), refs = refs[:9], refs[9:]
    (table_sem, recv1, recv2, y_sem, send1, send2, send_u, recv_u, send_s, recv_s, send_t, recv_t) = refs

    sd, cols = x_ref.shape
    rows = 2 * nh
    cb = modes * cols // nc
    nblk = cols // cb
    tiles = sd // 8
    me = lax.axis_index("ctx")
    my = lax.axis_index("ch")

    near = min(nc, 16)
    spread = nc // near
    across = min(nh, 4)
    zs = near // 2
    far_y = sorted(range(spread), key=lambda d: -min(d, spread - d))
    far_x = sorted(range(across), key=lambda d: -min(d, across - d))
    ch_steps = [(d, e) for d in far_x for e in range(nh // across - 1, -1, -1)][:-1]
    group = me // near

    def group_of(dy):
        return lax.rem(group + dy, spread)

    def ctx_peer(dy, t):
        m = t // 2
        dz = zs // 2 + ((m + 1) // 2) * (2 * (m % 2) - 1) + zs
        z = lax.rem(lax.rem(me, near) // 2 + dz, zs)
        core = lax.rem(me + 1 - t % 2, 2)
        return group_of(dy) * near + z * 2 + core

    def ch_peer(step):
        dx, dy = step
        return lax.rem(my // across + dy, nh // across) * across + lax.rem(my + dx, across)

    def each_ctx(dy, act):
        def body(t, _):
            act(ctx_peer(dy, t))
            return 0

        lax.fori_loop(0, near if dy else near - 1, body, 0)

    barrier = pltpu.get_barrier_semaphore()

    def greet(peer):
        pl.semaphore_signal(barrier, inc=1, device_id={"ctx": peer}, device_id_type=MESH)

    loads = [
        pltpu.make_async_copy(src, dst, table_sem.at[n]) for n, (src, dst) in enumerate(zip(args_in, args))
    ]
    for load in loads:
        load.start()

    for n, dy in enumerate(far_y):
        each_ctx(dy, greet)
        if n == 0:
            for step in ch_steps:
                pl.semaphore_signal(barrier, inc=1, device_id={"ch": ch_peer(step)}, device_id_type=MESH)

    width = min(cols, 256)
    eye = (
        lax.broadcasted_iota(jnp.int32, (width, width), 0)
        == lax.broadcasted_iota(jnp.int32, (width, width), 1)
    ).astype(F32).astype(BF16)
    for arr, ref in enumerate((x_ref, g_ref)):
        loads[arr].wait()
        for c0 in range(0, cols, width):
            turned = lax.dot_general(
                eye, ref[:, c0 : c0 + width], (((1,), (1,)), ((), ())), preferred_element_type=F32
            ).astype(BF16)
            for k in range(width // near):
                c = c0 + k * near
                s1[c // nc, c % nc // near, arr] = turned[k * near : (k + 1) * near]

    pl.semaphore_wait(barrier, nh - 1 + nc - 1)

    def ch_copy(step, src, dst, n):
        return pltpu.make_async_remote_copy(
            src_ref=src,
            dst_ref=dst,
            send_sem=send1,
            recv_sem=recv1.at[n],
            device_id={"ch": ch_peer(step)},
            device_id_type=MESH,
        )

    for n, dy in enumerate(far_y):
        for step in ch_steps:
            ch_copy(step, s1.at[ch_peer(step), group_of(dy)], r1.at[my, group_of(dy)], n).start()
    r1[pl.ds(my, 1)] = s1[pl.ds(my, 1)]

    for n in (2, 3, 4):
        loads[n].wait()

    grad[...] = g_ref[...].astype(F32)
    eight = lax.broadcasted_iota(jnp.int32, (8, cb), 0).astype(F32)
    octs = 8.0 * lax.broadcasted_iota(jnp.int32, (tiles, cb), 0).astype(F32)

    def weight_of(rate, residue):
        x = 2.0 * rate
        series = 1.0 - x * (1.0 / 7.0)
        for n in (6, 5, 4, 3, 2):
            series = 1.0 - (x * (1.0 / n)) * series
        return residue * jnp.sqrt(x * series)

    def columns(blk):
        return pl.ds(pl.multiple_of(blk * cb, cb), cb)

    def states(blk, _):
        at = columns(blk)
        rate = rate_ref[:, at]
        weight = weight_of(rate, res_ref[:, at])
        ww[:, at] = weight
        for n in range(modes):
            slow = jnp.exp(-rate[n : n + 1] * octs)
            eb[n] = slow
        fine = [jnp.exp(-rate[n : n + 1] * eight) for n in range(modes)]
        scaled = [fine[n] * weight[n : n + 1] for n in range(modes)]
        sums = [jnp.zeros((8, cb), F32) for _ in range(modes)]
        for t in range(tiles):
            g = grad[8 * t : 8 * t + 8, at]
            tap = jnp.zeros((8, cb), F32)
            for n in range(modes):
                level = jnp.broadcast_to(eb[n, t : t + 1], (8, cb))
                sums[n] = sums[n] + level * g
                tap = tap + level * scaled[n]
            taps[8 * t : 8 * t + 8, at] = tap
        for n in range(modes):
            rate_rows[n * nblk + blk] = rate[n : n + 1]
            u_own[n * nblk + blk] = jnp.sum(sums[n] * fine[n], axis=0, keepdims=True)
        return 0

    lax.fori_loop(0, nblk, states, 0)

    def ctx_copy(peer, src, dst, send, recv):
        return pltpu.make_async_remote_copy(
            src_ref=src, dst_ref=dst, send_sem=send, recv_sem=recv, device_id={"ctx": peer}, device_id_type=MESH
        )

    def send_to_ctx(own, everyone, send, recv):
        for dy in far_y:
            each_ctx(dy, lambda peer: ctx_copy(peer, own.at[peer], everyone.at[me], send, recv).start())
        everyone[pl.ds(me, 1)] = own[pl.ds(me, 1)]

    def wait_ctx(own, everyone, send, recv, count=nc - 1):
        return ctx_copy(ctx_peer(0, 0), own.at[pl.ds(0, count)], everyone.at[pl.ds(0, count)], send, recv)

    send_to_ctx(u_own, u_all, send_u, recv_u)

    for n, dy in enumerate(far_y):
        ch_copy(ch_steps[0], s1.at[pl.ds(0, nh - 1), 0], r1.at[pl.ds(0, nh - 1), 0], n).wait_recv()
        if n == 0:
            loads[5].wait()
        block = r1[:, pl.ds(group_of(dy), 1)].reshape(rows * near, sd)
        s2[pl.ds(group_of(dy) * near, near)] = dot(perm[...], block).astype(BF16).reshape(near, rows, sd)
        each_ctx(dy, lambda peer: ctx_copy(peer, s2.at[peer], r2.at[me], send2, recv2.at[group]).start())
    r2[pl.ds(me, 1)] = s2[pl.ds(me, 1)]

    wait_ctx(u_own, u_all, send_u, recv_u).wait_recv()
    decay = jnp.exp(-rate_rows[me] * float(sd))
    state = jnp.zeros((1, cb), F32)
    for p in range(nc - 1, -1, -1):
        st_own[p] = state
        state = u_all[p] + decay * state
    send_to_ctx(st_own, st_all, send_s, recv_s)

    loads[11].wait()
    loads[12].wait()
    wide = min(cols, 256)

    def inside(blk, _):
        at = pl.ds(pl.multiple_of(blk * wide, wide), wide)
        g = g_ref[:, at]
        g_spec = dot(near_in[:, : 2 * sd], jnp.concatenate([g, g], axis=0))
        high, low = split(taps[:, at])
        h_spec = dot(near_in[...], jnp.concatenate([high, high, low], axis=0))
        g_re, g_im = g_spec[:sd], g_spec[sd:]
        h_re, h_im = h_spec[:sd], h_spec[sd:]
        term = jnp.concatenate([h_re * g_re + h_im * g_im, h_re * g_im - h_im * g_re], axis=0)
        high, low = split(term)
        part = dot(near_out[...], jnp.concatenate([high, low, high], axis=0)) * (1.0 / sd)
        y[:, at] = part + gain_ref[:, at] * grad[:, at]
        return 0

    lax.fori_loop(0, cols // wide, inside, 0)

    for n in (6, 7, 8, 9, 10):
        loads[n].wait()
    for dy in reversed(far_y):
        wait_ctx(s2, r2, send2, recv2.at[group_of(dy)], near if dy else near - 1).wait_recv()
        block = r2[pl.ds(group_of(dy) * near, near)].reshape(near * rows, sd)
        blocks[pl.ds(group_of(dy), 1)] = dot(perm_t[...], block).astype(BF16).reshape(1, rows, near, sd)
    turn_c, turn_s = twist[0], twist[1]
    spec[...] = jnp.zeros_like(spec)

    def pair(q, _):
        for k in range(4):
            part = [blocks[a, 4 * q + k] for a in range(spread)]
            freq = dot(first[...], jnp.concatenate(part + part, axis=0))
            re, im = freq[:nc], freq[nc:]
            high_re, low_re = split(re * turn_c + im * turn_s)
            high_im, low_im = split(im * turn_c - re * turn_s)
            at = pl.ds(((k % 2) * 2 + k // 2) * nc, nc)
            for n, piece in enumerate((high_re, high_im, low_re, low_im, high_re, high_im)):
                left[at, n * sd : (n + 1) * sd] = piece
        both = dot(left[...], second[...])
        x_re, x_im = both[: 2 * nc, :sd], both[: 2 * nc, sd:]
        g_re, g_im = both[2 * nc :, :sd], both[2 * nc :, sd:]
        re = x_re * g_re + x_im * g_im
        im = x_re * g_im - x_im * g_re
        spec[:, :sd] += re[:nc] + re[nc:]
        spec[:, sd:] += im[:nc] + im[nc:]
        return 0

    lax.fori_loop(0, nh // 2, pair, 0)

    re_h, re_l = split(spec[:, :sd])
    im_h, im_l = split(-spec[:, sd:])
    both = dot(jnp.concatenate([re_h, im_h, re_l, im_l, re_h, im_h], axis=1), second[...])
    re, im = both[:, :sd], -both[:, sd:]
    high, low = split(
        jnp.concatenate([re * turn_c - im * turn_s, im * turn_c + re * turn_s], axis=0)
    )
    scale = 2.0 / (2 * nc * sd) / math.sqrt(nc * sd * nh)
    result = dot(last[...], jnp.concatenate([high, low, high], axis=0)) * scale
    for d in range(nc):
        t_own[d] = result[d : d + 1]
    send_to_ctx(t_own, t_all, send_t, recv_t)

    wait_ctx(st_own, st_all, send_s, recv_s).wait_recv()

    def outside(blk, _):
        at = columns(blk)
        rate = rate_ref[:, at]
        weight = ww[:, at]
        fine = []
        for n in range(modes):
            carried = weight[n : n + 1] * st_all[n * nblk + blk]
            eb[n] = carried * jnp.exp(-rate[n : n + 1] * (float(sd - 8) - octs))
            fine.append(jnp.exp(-rate[n : n + 1] * (8.0 - eight)))
        for t in range(tiles):
            total = y[8 * t : 8 * t + 8, at]
            for n in range(modes):
                total = total + jnp.broadcast_to(eb[n, t : t + 1], (8, cb)) * fine[n]
            y[8 * t : 8 * t + 8, at] = total
        return 0

    lax.fori_loop(0, nblk, outside, 0)

    leave = pltpu.make_async_copy(y, y_ref, y_sem)
    leave.start()

    wait_ctx(t_own, t_all, send_t, recv_t).wait_recv()
    gathered = jnp.concatenate([t_all[d] for d in range(nc)], axis=0)
    out_ref[...] = gathered

    leave.wait()
    ch_copy(ch_steps[0], s1.at[pl.ds(0, nh - 1)], r1.at[pl.ds(0, nh - 1)], 0).wait_send()
    wait_ctx(s2, r2, send2, recv2.at[0]).wait_send()
    wait_ctx(u_own, u_all, send_u, recv_u).wait_send()
    wait_ctx(st_own, st_all, send_s, recv_s).wait_send()
    wait_ctx(t_own, t_all, send_t, recv_t).wait_send()


def body(nc, nh, inputs, out_grad, decay_rate, residue, skip_gain):
    sd, cols = inputs.shape
    modes = decay_rate.shape[0]
    rows = 2 * nh
    cb = modes * cols // nc
    args = (inputs, out_grad, decay_rate, residue, skip_gain.reshape(1, cols))
    args += tuple(jnp.asarray(t) for t in tables(nc, nh, sd))
    near = min(nc, 16)
    spread = nc // near
    vmem = pl.BlockSpec(memory_space=pltpu.VMEM)
    dma = pltpu.SemaphoreType.DMA
    input_grad, filter_grad = pl.pallas_call(
        functools.partial(kernel, nc, nh, modes),
        out_shape=(
            jax.ShapeDtypeStruct((sd, cols), F32),
            jax.ShapeDtypeStruct((nc, sd), F32),
        ),
        in_specs=[pl.BlockSpec(memory_space=pltpu.HBM)] * len(args),
        out_specs=(pl.BlockSpec(memory_space=pltpu.HBM), vmem),
        scratch_shapes=[pltpu.VMEM(arg.shape, arg.dtype) for arg in args]
        + [
            pltpu.VMEM((nh, spread, 2, near, sd), BF16),
            pltpu.VMEM((nh, spread, 2, near, sd), BF16),
            pltpu.VMEM((nc, rows, sd), BF16),
            pltpu.VMEM((nc, rows, sd), BF16),
            pltpu.VMEM((nc, 1, cb), F32),
            pltpu.VMEM((nc, 1, cb), F32),
            pltpu.VMEM((nc, 1, cb), F32),
            pltpu.VMEM((nc, 1, cb), F32),
            pltpu.VMEM((nc, 1, sd), F32),
            pltpu.VMEM((nc, 1, sd), F32),
            pltpu.VMEM((sd, cols), F32),
            pltpu.VMEM((sd, cols), F32),
            pltpu.VMEM((sd, cols), F32),
            pltpu.VMEM((modes, sd // 8, cb), F32),
            pltpu.VMEM((modes, cols), F32),
            pltpu.VMEM((nc, 1, cb), F32),
            pltpu.VMEM((spread, rows, near, sd), BF16),
            pltpu.VMEM((4 * nc, 6 * sd), BF16),
            pltpu.VMEM((nc, 2 * sd), F32),
            dma((len(args),)),
            dma((spread,)),
            dma((spread,)),
        ]
        + [dma] * 9,
        compiler_params=pltpu.CompilerParams(
            collective_id=0, has_side_effects=True, vmem_limit_bytes=64 * 1024 * 1024
        ),
        name="modal_backward",
    )(*args)
    return input_grad, filter_grad.T


def solution(mesh):
    placed = (P("ctx", "ch"), P("ctx", "ch"), P(), P(), P("ch"))
    return jax.shard_map(
        functools.partial(body, mesh.shape["ctx"], mesh.shape["ch"]),
        mesh=mesh,
        in_specs=placed,
        out_specs=(P("ctx", "ch"), P("ctx", "ch")),
        check_vma=False,
    )
```

```python
import functools
import math

import jax
import jax.numpy as jnp
import ml_dtypes
import numpy as np
from jax import lax
from jax.experimental import pallas as pl
from jax.experimental.pallas import tpu as pltpu
from jax.sharding import PartitionSpec as P

MESH = pl.DeviceIdType.MESH
F32 = jnp.float32
BF16 = jnp.bfloat16


def shape_of(nc, nh):
    z = nc // 8 if nc >= 32 else nc // 4
    x = nh // 2
    return nc // (2 * z), z, 2, nh // x, x


def halves(table):
    high = table.astype(np.float32).astype(ml_dtypes.bfloat16)
    low = (table - high.astype(np.float64)).astype(np.float32).astype(ml_dtypes.bfloat16)
    return high, low


@functools.lru_cache(maxsize=None)
def tables(nc, nh, sd):
    _, zs, cores, _, xs = shape_of(nc, nh)
    j = np.arange(nc) + 0.5
    a = np.arange(nc)
    s = np.arange(sd)
    full = 2 * nc * sd
    angle = 2.0 * np.pi * np.outer(j, a) / (2 * nc)
    block = np.concatenate([np.cos(angle), -np.sin(angle)], axis=0)
    high, low = halves(block)
    first = np.concatenate([high, low], axis=1)
    last_h, last_l = halves(block.T.copy())
    last = np.concatenate([last_h, last_h, last_l], axis=1)
    angle = 2.0 * np.pi * np.outer(j, s) / full
    twist = np.stack([np.cos(angle), np.sin(angle)]).astype(np.float32)
    angle = 2.0 * np.pi * (np.outer(s, s) % sd) / sd
    cos, sin = np.cos(angle), np.sin(angle)
    step = np.concatenate([np.concatenate([cos, -sin], axis=1), np.concatenate([sin, cos], axis=1)], axis=0)
    high, low = halves(step)
    second = np.concatenate([high, high, low], axis=0)
    angle = 2.0 * np.pi * np.outer(s + 0.5, s) / (2 * sd)
    near = np.concatenate([np.cos(angle), -np.sin(angle)], axis=0)
    high, low = halves(near)
    near_in = np.concatenate([high, low, high], axis=1)
    near_out = np.concatenate([high.T, high.T, low.T], axis=1)
    rows = cores * xs * 2
    gather = np.zeros((zs * rows, zs * rows), np.float32)
    spread = np.zeros((zs * rows, zs * rows), np.float32)
    for z in range(zs):
        for q in range(cores * xs):
            for arr in range(2):
                gather[(z * cores * xs + q) * 2 + arr, (q * 2 + arr) * zs + z] = 1.0
                core, x = q // xs, q % xs
                spread[((x * 2 + arr) * zs + z) * cores + core, (z * cores * xs + q) * 2 + arr] = 1.0
    bf = ml_dtypes.bfloat16
    return (
        gather.astype(bf),
        spread.astype(bf),
        first,
        np.ascontiguousarray(second),
        last,
        twist,
        near_in,
        np.ascontiguousarray(near_out),
    )


def split(value):
    high = value.astype(BF16)
    return high, (value - high.astype(F32)).astype(BF16)


def dot(left, right):
    return jnp.dot(left, right, preferred_element_type=F32)


def kernel(nc, nh, modes, *refs):
    args_in, refs = refs[:13], refs[13:]
    (y_ref, out_ref), refs = refs[:2], refs[2:]
    args, refs = refs[:13], refs[13:]
    x_ref, g_ref, rate_ref, res_ref, gain_ref, gather, spread, first, second, last, twist, near_in, near_out = args
    (s1, r1, s2, r2, u_own, u_all, st_own, st_all, t_own, t_all), refs = refs[:10], refs[10:]
    (y, grad, taps, eb, ww, rate_rows, blocks, left, spec), refs = refs[:9], refs[9:]
    (table_sem, recv1, recv2, y_sem, send1, send2, send_u, recv_u, send_s, recv_s, send_t, recv_t) = refs

    sd, cols = x_ref.shape
    cb = modes * cols // nc
    nblk = cols // cb
    tiles = sd // 8
    yhs, zs, cores, yls, xs = shape_of(nc, nh)
    ys, qs, run = yhs * yls, cores * xs, zs * cores
    me = lax.axis_index("ctx")
    my = lax.axis_index("ch")
    yh, z, core = me // run, lax.rem(me, run) // cores, lax.rem(me, cores)
    yl, x = my // xs, lax.rem(my, xs)
    y_me = yh * yls + yl
    q_me = core * xs + x

    def farthest(count):
        return sorted(range(count), key=lambda d: -min(d, count - d))

    far_y = farthest(ys)
    q_steps = [(dc, dx) for dx in farthest(xs) for dc in (1, 0)][:-1]

    def z_at(m):
        return lax.rem(z + zs // 2 + ((m + 1) // 2) * (2 * lax.rem(m, 2) - 1) + zs, zs)

    def y_at(dy):
        return lax.rem(y_me + dy, ys)

    def plane_peer(dy, m):
        there = y_at(dy)
        device = {"ctx": (there // yls * zs + z_at(m)) * cores + core, "ch": lax.rem(there, yls) * xs + x}
        return device, there * zs + z_at(m)

    def chip_peer(step):
        dc, dx = step
        core_at, x_at = lax.rem(core + dc, cores), lax.rem(x + dx, xs)
        return {"ctx": me - core + core_at, "ch": yl * xs + x_at}, core_at * xs + x_at

    def ctx_peer(dyh, t):
        return (lax.rem(yh + dyh, yhs) * zs + z_at(t // cores)) * cores + lax.rem(core + 1 - lax.rem(t, cores), cores)

    def each_plane(dy, act):
        def body(m, _):
            act(*plane_peer(dy, m))
            return 0

        lax.fori_loop(0, zs if dy else zs - 1, body, 0)

    def each_ctx(dyh, act):
        def body(t, _):
            act(ctx_peer(dyh, t))
            return 0

        lax.fori_loop(0, run if dyh else run - 1, body, 0)

    barrier = pltpu.get_barrier_semaphore()

    def greet(device, _):
        pl.semaphore_signal(barrier, inc=1, device_id=device, device_id_type=MESH)

    loads = [
        pltpu.make_async_copy(src, dst, table_sem.at[n]) for n, (src, dst) in enumerate(zip(args_in, args))
    ]
    for load in loads:
        load.start()

    for n, dy in enumerate(far_y):
        each_plane(dy, greet)
        if n == 2:
            for step in q_steps:
                greet(*chip_peer(step))

    for dyh in farthest(yhs):
        def other(m, _):
            device = (lax.rem(yh + dyh, yhs) * zs + z_at(m)) * cores + lax.rem(core + 1, cores)
            greet({"ctx": device}, 0)
            return 0

        lax.fori_loop(0, zs if dyh else zs - 1, other, 0)

    width = min(cols, 256)
    row = lax.broadcasted_iota(jnp.int32, (width, width), 0)
    turn = (
        (row & -run) + (row & (zs - 1)) * cores + ((row & (run - 1)) // zs)
        == lax.broadcasted_iota(jnp.int32, (width, width), 1)
    ).astype(F32).astype(BF16)
    loads[0].wait()
    loads[1].wait()
    for c0 in range(0, cols, width):
        pair_of = [
            lax.dot_general(turn, ref[:, c0 : c0 + width], (((1,), (1,)), ((), ())), preferred_element_type=F32)
            for ref in (x_ref, g_ref)
        ]
        for r0 in range(0, width, zs):
            c = c0 + r0
            to_core = c % run // zs
            to_yh = c // run % yhs
            to_yl, to_x = c // nc // xs, c // nc % xs
            both = jnp.concatenate([part[r0 : r0 + zs] for part in pair_of], axis=0)
            s1[to_core * xs + to_x, to_yh * yls + to_yl] = both.astype(BF16)

    pl.semaphore_wait(barrier, (ys * zs - 1) + (qs - 1) + (yhs * zs - 1))

    def copy(device, src, dst, send, recv):
        return pltpu.make_async_remote_copy(
            src_ref=src, dst_ref=dst, send_sem=send, recv_sem=recv, device_id=device, device_id_type=MESH
        )

    some_chip, _ = chip_peer(q_steps[0])
    for n, dy in enumerate(far_y):
        for step in q_steps:
            device, q_at = chip_peer(step)
            copy(device, s1.at[q_at, y_at(dy)], r1.at[q_me, y_at(dy)], send1, recv1.at[n]).start()
    r1[pl.ds(q_me, 1)] = s1[pl.ds(q_me, 1)]

    for n in (2, 3, 4):
        loads[n].wait()

    grad[...] = g_ref[...].astype(F32)
    eight = lax.broadcasted_iota(jnp.int32, (8, cb), 0).astype(F32)
    octs = 8.0 * lax.broadcasted_iota(jnp.int32, (tiles, cb), 0).astype(F32)

    def weight_of(rate, residue):
        x = 2.0 * rate
        series = 1.0 - x * (1.0 / 7.0)
        for n in (6, 5, 4, 3, 2):
            series = 1.0 - (x * (1.0 / n)) * series
        return residue * jnp.sqrt(x * series)

    def columns(blk):
        return pl.ds(pl.multiple_of(blk * cb, cb), cb)

    def states(blk, _):
        at = columns(blk)
        rate = rate_ref[:, at]
        weight = weight_of(rate, res_ref[:, at])
        ww[:, at] = weight
        for n in range(modes):
            slow = jnp.exp(-rate[n : n + 1] * octs)
            eb[n] = slow
        fine = [jnp.exp(-rate[n : n + 1] * eight) for n in range(modes)]
        scaled = [fine[n] * weight[n : n + 1] for n in range(modes)]
        sums = [jnp.zeros((8, cb), F32) for _ in range(modes)]
        for t in range(tiles):
            g = grad[8 * t : 8 * t + 8, at]
            tap = jnp.zeros((8, cb), F32)
            for n in range(modes):
                level = jnp.broadcast_to(eb[n, t : t + 1], (8, cb))
                sums[n] = sums[n] + level * g
                tap = tap + level * scaled[n]
            taps[8 * t : 8 * t + 8, at] = tap
        for n in range(modes):
            rate_rows[n * nblk + blk] = rate[n : n + 1]
            u_own[n * nblk + blk] = jnp.sum(sums[n] * fine[n], axis=0, keepdims=True)
        return 0

    lax.fori_loop(0, nblk, states, 0)

    def ctx_copy(peer, src, dst, send, recv):
        return copy({"ctx": peer}, src, dst, send, recv)

    def send_to_ctx(own, everyone, send, recv):
        for dyh in farthest(yhs):
            each_ctx(dyh, lambda peer: ctx_copy(peer, own.at[peer], everyone.at[me], send, recv).start())
        everyone[pl.ds(me, 1)] = own[pl.ds(me, 1)]

    def wait_ctx(own, everyone, send, recv, count=nc - 1):
        return ctx_copy(ctx_peer(0, 0), own.at[pl.ds(0, count)], everyone.at[pl.ds(0, count)], send, recv)

    send_to_ctx(u_own, u_all, send_u, recv_u)

    for n, dy in enumerate(far_y):
        copy(some_chip, s1.at[pl.ds(0, qs - 1), 0], r1.at[pl.ds(0, qs - 1), 0], send1, recv1.at[n]).wait_recv()
        if n == 0:
            loads[5].wait()
        block = r1[:, pl.ds(y_at(dy), 1)].reshape(qs * 2 * zs, sd)
        s2[pl.ds(y_at(dy) * zs, zs)] = dot(gather[...], block).astype(BF16).reshape(zs, qs * 2, sd)

        def onward(device, at):
            copy(device, s2.at[at], r2.at[y_me * zs + z], send2, recv2.at[y_me]).start()

        each_plane(dy, onward)
    own = pl.ds(y_me * zs + z, 1)
    r2[own] = s2[own]

    wait_ctx(u_own, u_all, send_u, recv_u).wait_recv()
    decay = jnp.exp(-rate_rows[me] * float(sd))
    state = jnp.zeros((1, cb), F32)
    for p in range(nc - 1, -1, -1):
        st_own[p] = state
        state = u_all[p] + decay * state
    send_to_ctx(st_own, st_all, send_s, recv_s)

    loads[11].wait()
    loads[12].wait()
    wide = min(cols, 256)

    def inside(blk, _):
        at = pl.ds(pl.multiple_of(blk * wide, wide), wide)
        g = g_ref[:, at]
        g_spec = dot(near_in[:, : 2 * sd], jnp.concatenate([g, g], axis=0))
        high, low = split(taps[:, at])
        h_spec = dot(near_in[...], jnp.concatenate([high, high, low], axis=0))
        g_re, g_im = g_spec[:sd], g_spec[sd:]
        h_re, h_im = h_spec[:sd], h_spec[sd:]
        term = jnp.concatenate([h_re * g_re + h_im * g_im, h_re * g_im - h_im * g_re], axis=0)
        high, low = split(term)
        part = dot(near_out[...], jnp.concatenate([high, low, high], axis=0)) * (1.0 / sd)
        y[:, at] = part + gain_ref[:, at] * grad[:, at]
        return 0

    lax.fori_loop(0, cols // wide, inside, 0)

    for n in (6, 7, 8, 9, 10):
        loads[n].wait()
    some_plane, _ = plane_peer(far_y[0], 0)
    for dy in reversed(far_y):
        count = zs if dy else zs - 1
        copy(
            some_plane, s2.at[pl.ds(0, count)], r2.at[pl.ds(0, count)], send2, recv2.at[y_at(dy)]
        ).wait_recv()
        block = r2[pl.ds(y_at(dy) * zs, zs)].reshape(zs * qs * 2, sd)
        blocks[pl.ds(y_at(dy), 1)] = dot(spread[...], block).astype(BF16).reshape(1, xs * 2, run, sd)
    turn_c, turn_s = twist[0], twist[1]
    spec[...] = jnp.zeros_like(spec)

    def pair(q, _):
        for k in range(4):
            share = 2 * q + k // 2
            at = lax.rem(share, xs) * 2 + k % 2
            part = [blocks[a * yls + share // xs, at] for a in range(yhs)]
            freq = dot(first[...], jnp.concatenate(part + part, axis=0))
            re, im = freq[:nc], freq[nc:]
            high_re, low_re = split(re * turn_c + im * turn_s)
            high_im, low_im = split(im * turn_c - re * turn_s)
            at = pl.ds(((k % 2) * 2 + k // 2) * nc, nc)
            for n, piece in enumerate((high_re, high_im, low_re, low_im, high_re, high_im)):
                left[at, n * sd : (n + 1) * sd] = piece
        both = dot(left[...], second[...])
        x_re, x_im = both[: 2 * nc, :sd], both[: 2 * nc, sd:]
        g_re, g_im = both[2 * nc :, :sd], both[2 * nc :, sd:]
        re = x_re * g_re + x_im * g_im
        im = x_re * g_im - x_im * g_re
        spec[:, :sd] += re[:nc] + re[nc:]
        spec[:, sd:] += im[:nc] + im[nc:]
        return 0

    lax.fori_loop(0, nh // 2, pair, 0)

    re_h, re_l = split(spec[:, :sd])
    im_h, im_l = split(-spec[:, sd:])
    both = dot(jnp.concatenate([re_h, im_h, re_l, im_l, re_h, im_h], axis=1), second[...])
    re, im = both[:, :sd], -both[:, sd:]
    high, low = split(
        jnp.concatenate([re * turn_c - im * turn_s, im * turn_c + re * turn_s], axis=0)
    )
    scale = 2.0 / (2 * nc * sd) / math.sqrt(nc * sd * nh)
    result = dot(last[...], jnp.concatenate([high, low, high], axis=0)) * scale
    for d in range(nc):
        t_own[d] = result[d : d + 1]
    send_to_ctx(t_own, t_all, send_t, recv_t)

    wait_ctx(st_own, st_all, send_s, recv_s).wait_recv()

    def outside(blk, _):
        at = columns(blk)
        rate = rate_ref[:, at]
        weight = ww[:, at]
        fine = []
        for n in range(modes):
            carried = weight[n : n + 1] * st_all[n * nblk + blk]
            eb[n] = carried * jnp.exp(-rate[n : n + 1] * (float(sd - 8) - octs))
            fine.append(jnp.exp(-rate[n : n + 1] * (8.0 - eight)))
        for t in range(tiles):
            total = y[8 * t : 8 * t + 8, at]
            for n in range(modes):
                total = total + jnp.broadcast_to(eb[n, t : t + 1], (8, cb)) * fine[n]
            y[8 * t : 8 * t + 8, at] = total
        return 0

    lax.fori_loop(0, nblk, outside, 0)

    leave = pltpu.make_async_copy(y, y_ref, y_sem)
    leave.start()

    wait_ctx(t_own, t_all, send_t, recv_t).wait_recv()
    gathered = jnp.concatenate([t_all[d] for d in range(nc)], axis=0)
    out_ref[...] = gathered

    leave.wait()
    copy(some_chip, s1.at[pl.ds(0, qs - 1)], r1.at[pl.ds(0, qs - 1)], send1, recv1.at[0]).wait_send()
    rest = pl.ds(0, ys * zs - 1)
    copy(some_plane, s2.at[rest], r2.at[rest], send2, recv2.at[0]).wait_send()
    wait_ctx(u_own, u_all, send_u, recv_u).wait_send()
    wait_ctx(st_own, st_all, send_s, recv_s).wait_send()
    wait_ctx(t_own, t_all, send_t, recv_t).wait_send()


def finish(input_in, filter_in, input_out, filter_out):
    input_out[...] = input_in[...]
    filter_out[...] = filter_in[...]


def body(nc, nh, inputs, out_grad, decay_rate, residue, skip_gain):
    sd, cols = inputs.shape
    modes = decay_rate.shape[0]
    cb = modes * cols // nc
    args = (inputs, out_grad, decay_rate, residue, skip_gain.reshape(1, cols))
    args += tuple(jnp.asarray(t) for t in tables(nc, nh, sd))
    yhs, zs, cores, yls, xs = shape_of(nc, nh)
    ys, qs = yhs * yls, cores * xs
    vmem = pl.BlockSpec(memory_space=pltpu.VMEM)
    dma = pltpu.SemaphoreType.DMA
    input_grad, filter_grad = pl.pallas_call(
        functools.partial(kernel, nc, nh, modes),
        out_shape=(
            jax.ShapeDtypeStruct((sd, cols), F32),
            jax.ShapeDtypeStruct((nc, sd), F32),
        ),
        in_specs=[pl.BlockSpec(memory_space=pltpu.HBM)] * len(args),
        out_specs=(pl.BlockSpec(memory_space=pltpu.HBM), vmem),
        scratch_shapes=[pltpu.VMEM(arg.shape, arg.dtype) for arg in args]
        + [
            pltpu.VMEM((qs, ys, 2 * zs, sd), BF16),
            pltpu.VMEM((qs, ys, 2 * zs, sd), BF16),
            pltpu.VMEM((ys * zs, qs * 2, sd), BF16),
            pltpu.VMEM((ys * zs, qs * 2, sd), BF16),
            pltpu.VMEM((nc, 1, cb), F32),
            pltpu.VMEM((nc, 1, cb), F32),
            pltpu.VMEM((nc, 1, cb), F32),
            pltpu.VMEM((nc, 1, cb), F32),
            pltpu.VMEM((nc, 1, sd), F32),
            pltpu.VMEM((nc, 1, sd), F32),
            pltpu.VMEM((sd, cols), F32),
            pltpu.VMEM((sd, cols), F32),
            pltpu.VMEM((sd, cols), F32),
            pltpu.VMEM((modes, sd // 8, cb), F32),
            pltpu.VMEM((modes, cols), F32),
            pltpu.VMEM((nc, 1, cb), F32),
            pltpu.VMEM((ys, xs * 2, zs * cores, sd), BF16),
            pltpu.VMEM((4 * nc, 6 * sd), BF16),
            pltpu.VMEM((nc, 2 * sd), F32),
            dma((len(args),)),
            dma((ys,)),
            dma((ys,)),
        ]
        + [dma] * 9,
        compiler_params=pltpu.CompilerParams(
            collective_id=0, has_side_effects=True, vmem_limit_bytes=64 * 1024 * 1024
        ),
        name="modal_backward",
    )(*args)
    input_grad, filter_grad = pl.pallas_call(
        finish,
        out_shape=(jax.ShapeDtypeStruct((sd, cols), F32), jax.ShapeDtypeStruct((nc, sd), F32)),
        in_specs=[vmem, vmem],
        out_specs=(vmem, vmem),
        compiler_params=pltpu.CompilerParams(vmem_limit_bytes=64 * 1024 * 1024),
        name="finish",
    )(input_grad, filter_grad)
    return input_grad, filter_grad.T


def solution(mesh):
    placed = (P("ctx", "ch"), P("ctx", "ch"), P(), P(), P("ch"))
    return jax.shard_map(
        functools.partial(body, mesh.shape["ctx"], mesh.shape["ch"]),
        mesh=mesh,
        in_specs=placed,
        out_specs=(P("ctx", "ch"), P("ctx", "ch")),
        check_vma=False,
    )
```

```python
import functools
import math

import jax
import jax.numpy as jnp
import ml_dtypes
import numpy as np
from jax import lax
from jax.experimental import pallas as pl
from jax.experimental.pallas import tpu as pltpu
from jax.sharding import PartitionSpec as P

MESH = pl.DeviceIdType.MESH
F32 = jnp.float32
BF16 = jnp.bfloat16


def shape_of(nc, nh):
    z = nc // 8 if nc >= 32 else nc // 4
    x = nh // 2
    return nc // (2 * z), z, 2, nh // x, x


def halves(table):
    high = table.astype(np.float32).astype(ml_dtypes.bfloat16)
    low = (table - high.astype(np.float64)).astype(np.float32).astype(ml_dtypes.bfloat16)
    return high, low


def reorder(sizes, old, new):
    count = np.arange(math.prod(sizes[axis] for axis in old)).reshape([sizes[axis] for axis in old])
    moved = count.transpose([old.index(axis) for axis in new]).reshape(-1)
    return np.eye(moved.size, dtype=np.float32)[moved]


@functools.lru_cache(maxsize=None)
def tables(nc, nh, sd):
    _, zs, cores, _, xs = shape_of(nc, nh)
    j = np.arange(nc) + 0.5
    a = np.arange(nc)
    s = np.arange(sd)
    full = 2 * nc * sd
    angle = 2.0 * np.pi * np.outer(j, a) / (2 * nc)
    block = np.concatenate([np.cos(angle), -np.sin(angle)], axis=0)
    high, low = halves(block)
    first = np.concatenate([high, low], axis=1)
    last_h, last_l = halves(block.T.copy())
    last = np.concatenate([last_h, last_h, last_l], axis=1)
    angle = 2.0 * np.pi * np.outer(j, s) / full
    twist = np.stack([np.cos(angle), np.sin(angle)]).astype(np.float32)
    angle = 2.0 * np.pi * (np.outer(s, s) % sd) / sd
    cos, sin = np.cos(angle), np.sin(angle)
    step = np.concatenate([np.concatenate([cos, -sin], axis=1), np.concatenate([sin, cos], axis=1)], axis=0)
    high, low = halves(step)
    second = np.concatenate([high, high, low], axis=0)
    angle = 2.0 * np.pi * np.outer(s + 0.5, s) / (2 * sd)
    near = np.concatenate([np.cos(angle), -np.sin(angle)], axis=0)
    high, low = halves(near)
    near_in = np.concatenate([high, low, high], axis=1)
    near_out = np.concatenate([high.T, high.T, low.T], axis=1)
    qx = {"q": cores * xs, "core": cores, "x": xs, "arr": 2, "z": zs}
    moves = [
        reorder(qx, ("core", "x", "arr", "z"), ("z", "core", "x", "arr")),
        reorder(qx, ("z", "core", "x", "arr"), ("x", "arr", "z", "core")),
        reorder(qx, ("arr", "x", "core", "z"), ("z", "arr", "core", "x")),
        reorder(qx, ("z", "arr", "core", "x"), ("core", "x", "arr", "z")),
        reorder(qx, ("core", "x", "arr", "z"), ("x", "arr", "z", "core")),
    ]
    bf = ml_dtypes.bfloat16
    return (
        np.stack(moves).astype(bf),
        first,
        np.ascontiguousarray(second),
        last,
        twist,
        near_in,
        np.ascontiguousarray(near_out),
    )


def split(value):
    high = value.astype(BF16)
    return high, (value - high.astype(F32)).astype(BF16)


def dot(left, right):
    return jnp.dot(left, right, preferred_element_type=F32)


def kernel(nc, nh, modes, *refs):
    args_in, refs = refs[:12], refs[12:]
    (y_ref, out_ref), refs = refs[:2], refs[2:]
    args, refs = refs[:12], refs[12:]
    x_ref, g_ref, rate_ref, res_ref, gain_ref, moves, first, second, last, twist, near_in, near_out = args
    (runs, s1, r1, s2, r2, s3, r3, s4, r4), refs = refs[:9], refs[9:]
    (u_own, u_all, st_own, st_all, t_own, t_all), refs = refs[:6], refs[6:]
    (y, grad, taps, eb, ww, rate_rows, blocks, left, spec), refs = refs[:9], refs[9:]
    (table_sem, recv1, recv2, recv3, recv4, y_sem, send1, send2, send3, send4, send_u, recv_u, send_s, recv_s, send_t, recv_t) = refs

    sd, cols = x_ref.shape
    cb = modes * cols // nc
    nblk = cols // cb
    tiles = sd // 8
    yhs, zs, cores, yls, xs = shape_of(nc, nh)
    ys, qs, run = yhs * yls, cores * xs, zs * cores
    me = lax.axis_index("ctx")
    my = lax.axis_index("ch")
    yh, z, core = me // run, lax.rem(me, run) // cores, lax.rem(me, cores)
    yl, x = my // xs, lax.rem(my, xs)
    y_me = yh * yls + yl
    q_me = core * xs + x

    def farthest(count):
        return sorted(range(count), key=lambda d: -min(d, count - d))

    far_y = farthest(ys)
    even = [dy for dy in far_y if dy % yls == 0]
    odd = [dy for dy in far_y if dy % yls]
    q_steps = [(dc, dx) for dx in farthest(xs) for dc in (1, 0)][:-1]

    def z_at(m):
        return lax.rem(z + zs // 2 + ((m + 1) // 2) * (2 * lax.rem(m, 2) - 1) + zs, zs)

    def y_at(dy):
        return lax.rem(y_me + dy, ys)

    def plane_peer(dy, m):
        there = y_at(dy)
        device = {"ctx": (there // yls * zs + z_at(m)) * cores + core, "ch": lax.rem(there, yls) * xs + x}
        return device, there * zs + z_at(m)

    def chip_peer(step):
        dc, dx = step
        core_at, x_at = lax.rem(core + dc, cores), lax.rem(x + dx, xs)
        return {"ctx": me - core + core_at, "ch": yl * xs + x_at}, core_at * xs + x_at

    def ctx_peer(dyh, t):
        return (lax.rem(yh + dyh, yhs) * zs + z_at(t // cores)) * cores + lax.rem(core + 1 - lax.rem(t, cores), cores)

    def each_plane(dy, act):
        def body(m, _):
            act(*plane_peer(dy, m))
            return 0

        lax.fori_loop(0, zs if dy else zs - 1, body, 0)

    def each_ctx(dyh, act):
        def body(t, _):
            act(ctx_peer(dyh, t))
            return 0

        lax.fori_loop(0, run if dyh else run - 1, body, 0)

    barrier = pltpu.get_barrier_semaphore()

    def greet(device, _):
        pl.semaphore_signal(barrier, inc=1, device_id=device, device_id_type=MESH)

    loads = [
        pltpu.make_async_copy(src, dst, table_sem.at[n]) for n, (src, dst) in enumerate(zip(args_in, args))
    ]
    for load in loads[:5]:
        load.start()

    for n, dy in enumerate(far_y):
        each_plane(dy, greet)
        if n == 2:
            for step in q_steps:
                greet(*chip_peer(step))

    for dyh in farthest(yhs):
        def other(m, _):
            device = (lax.rem(yh + dyh, yhs) * zs + z_at(m)) * cores + lax.rem(core + 1, cores)
            greet({"ctx": device}, 0)
            return 0

        lax.fori_loop(0, zs if dyh else zs - 1, other, 0)

    for load in loads[5:]:
        load.start()

    width = min(cols, 256)
    row = lax.broadcasted_iota(jnp.int32, (width, width), 0)
    turn = (
        (row & -run) + (row & (zs - 1)) * cores + ((row & (run - 1)) // zs)
        == lax.broadcasted_iota(jnp.int32, (width, width), 1)
    ).astype(F32).astype(BF16)
    loads[0].wait()
    loads[1].wait()
    for c0 in range(0, cols, width):
        pair_of = [
            lax.dot_general(turn, ref[:, c0 : c0 + width], (((1,), (1,)), ((), ())), preferred_element_type=F32)
            for ref in (x_ref, g_ref)
        ]
        for r0 in range(0, width, zs):
            c = c0 + r0
            to_core = c % run // zs
            to_yh = c // run % yhs
            to_yl, to_x = c // nc // xs, c // nc % xs
            both = jnp.concatenate([part[r0 : r0 + zs] for part in pair_of], axis=0)
            s1[to_core * xs + to_x, to_yh * yls + to_yl] = both.astype(BF16)
        for r0 in range(0, width, run):
            for arr in range(2):
                runs[arr, (c0 + r0) // run] = pair_of[arr][r0 : r0 + run].astype(BF16)
    loads[5].wait()
    for dy in odd:
        there = y_at(dy)
        first_run = lax.rem(there, yls) * xs * yhs + there // yls
        piece = [runs[arr, first_run + to_x * yhs] for arr in range(2) for to_x in range(xs)]
        piece = dot(moves[2], jnp.concatenate(piece, axis=0))
        s3[pl.ds(there * zs, zs)] = piece.astype(BF16).reshape(zs, qs * 2, sd)

    for n in (2, 3, 4):
        loads[n].wait()

    grad[...] = g_ref[...].astype(F32)
    eight = lax.broadcasted_iota(jnp.int32, (8, cb), 0).astype(F32)
    octs = 8.0 * lax.broadcasted_iota(jnp.int32, (tiles, cb), 0).astype(F32)

    def weight_of(rate, residue):
        x = 2.0 * rate
        series = 1.0 - x * (1.0 / 7.0)
        for n in (6, 5, 4, 3, 2):
            series = 1.0 - (x * (1.0 / n)) * series
        return residue * jnp.sqrt(x * series)

    def columns(blk):
        return pl.ds(pl.multiple_of(blk * cb, cb), cb)

    def states(blk, _):
        at = columns(blk)
        rate = rate_ref[:, at]
        weight = weight_of(rate, res_ref[:, at])
        ww[:, at] = weight
        for n in range(modes):
            slow = jnp.exp(-rate[n : n + 1] * octs)
            eb[n] = slow
        fine = [jnp.exp(-rate[n : n + 1] * eight) for n in range(modes)]
        scaled = [fine[n] * weight[n : n + 1] for n in range(modes)]
        sums = [jnp.zeros((8, cb), F32) for _ in range(modes)]
        for t in range(tiles):
            g = grad[8 * t : 8 * t + 8, at]
            tap = jnp.zeros((8, cb), F32)
            for n in range(modes):
                level = jnp.broadcast_to(eb[n, t : t + 1], (8, cb))
                sums[n] = sums[n] + level * g
                tap = tap + level * scaled[n]
            taps[8 * t : 8 * t + 8, at] = tap
        for n in range(modes):
            rate_rows[n * nblk + blk] = rate[n : n + 1]
            u_own[n * nblk + blk] = jnp.sum(sums[n] * fine[n], axis=0, keepdims=True)
        return 0

    lax.fori_loop(0, nblk, states, 0)

    def copy(device, src, dst, send, recv):
        return pltpu.make_async_remote_copy(
            src_ref=src, dst_ref=dst, send_sem=send, recv_sem=recv, device_id=device, device_id_type=MESH
        )

    some_chip, _ = chip_peer(q_steps[0])
    some_plane, _ = plane_peer(far_y[0], 0)
    def ctx_copy(peer, src, dst, send, recv):
        return copy({"ctx": peer}, src, dst, send, recv)

    def send_to_ctx(own, everyone, send, recv):
        for dyh in farthest(yhs):
            each_ctx(dyh, lambda peer: ctx_copy(peer, own.at[peer], everyone.at[me], send, recv).start())
        everyone[pl.ds(me, 1)] = own[pl.ds(me, 1)]

    def wait_ctx(own, everyone, send, recv, count=nc - 1):
        return ctx_copy(ctx_peer(0, 0), own.at[pl.ds(0, count)], everyone.at[pl.ds(0, count)], send, recv)

    pl.semaphore_wait(barrier, (ys * zs - 1) + (qs - 1) + (yhs * zs - 1))

    def to_chip(source, target, y, send, recv):
        for step in q_steps:
            device, q_at = chip_peer(step)
            copy(device, source.at[q_at, y], target.at[q_me, y], send, recv).start()
        target[pl.ds(q_me, 1), pl.ds(y, 1)] = source[pl.ds(q_me, 1), pl.ds(y, 1)]

    def to_plane(source, target, dy, send, recv):
        def onward(device, at):
            copy(device, source.at[at], target.at[y_me * zs + z], send, recv).start()

        each_plane(dy, onward)

    def wait_chip(source, target, send, recv):
        return copy(some_chip, source.at[pl.ds(0, qs - 1), 0], target.at[pl.ds(0, qs - 1), 0], send, recv)

    def wait_plane(source, target, count, send, recv):
        return copy(some_plane, source.at[pl.ds(0, count)], target.at[pl.ds(0, count)], send, recv)

    for n, dy in enumerate(even):
        to_chip(s1, r1, y_at(dy), send1, recv1.at[n])
    for dy in odd:
        to_plane(s3, r3, dy, send3, recv3.at[y_me])
    send_to_ctx(u_own, u_all, send_u, recv_u)

    for n, dy in enumerate(even):
        wait_chip(s1, r1, send1, recv1.at[n]).wait_recv()
        block = r1[:, pl.ds(y_at(dy), 1)].reshape(qs * 2 * zs, sd)
        s2[pl.ds(y_at(dy) * zs, zs)] = dot(moves[0], block).astype(BF16).reshape(zs, qs * 2, sd)
        to_plane(s2, r2, dy, send2, recv2.at[y_me])
    own = pl.ds(y_me * zs + z, 1)
    r2[own] = s2[own]

    loads[10].wait()
    loads[11].wait()
    wide = min(cols, 256)

    def inside(blk, _):
        at = pl.ds(pl.multiple_of(blk * wide, wide), wide)
        g = g_ref[:, at]
        g_spec = dot(near_in[:, : 2 * sd], jnp.concatenate([g, g], axis=0))
        high, low = split(taps[:, at])
        h_spec = dot(near_in[...], jnp.concatenate([high, high, low], axis=0))
        g_re, g_im = g_spec[:sd], g_spec[sd:]
        h_re, h_im = h_spec[:sd], h_spec[sd:]
        term = jnp.concatenate([h_re * g_re + h_im * g_im, h_re * g_im - h_im * g_re], axis=0)
        high, low = split(term)
        part = dot(near_out[...], jnp.concatenate([high, low, high], axis=0)) * (1.0 / sd)
        y[:, at] = part + gain_ref[:, at] * grad[:, at]
        return 0

    lax.fori_loop(0, cols // wide, inside, 0)

    wait_ctx(u_own, u_all, send_u, recv_u).wait_recv()
    decay = jnp.exp(-rate_rows[me] * float(sd))
    state = jnp.zeros((1, cb), F32)
    for p in range(nc - 1, -1, -1):
        st_own[p] = state
        state = u_all[p] + decay * state
    send_to_ctx(st_own, st_all, send_s, recv_s)

    for n, dy in enumerate(reversed(odd)):
        wait_plane(s3, r3, zs, send3, recv3.at[y_at(dy)]).wait_recv()
        block = r3[pl.ds(y_at(dy) * zs, zs)].reshape(zs * qs * 2, sd)
        s4[:, pl.ds(y_at(dy), 1)] = dot(moves[3], block).astype(BF16).reshape(qs, 1, 2 * zs, sd)
        to_chip(s4, r4, y_at(dy), send4, recv4.at[n])

    for n in (6, 7, 8, 9):
        loads[n].wait()
    turn_c, turn_s = twist[0], twist[1]

    def transform(part_of_y):
        total_re, total_im = 0.0, 0.0
        for q in range(xs // 2):
            for k in range(4):
                at = (2 * q + k // 2) * 2 + k % 2
                part = [blocks[a * yls + part_of_y, at] for a in range(yhs)]
                freq = dot(first[...], jnp.concatenate(part + part, axis=0))
                re, im = freq[:nc], freq[nc:]
                high_re, low_re = split(re * turn_c + im * turn_s)
                high_im, low_im = split(im * turn_c - re * turn_s)
                to = pl.ds(((k % 2) * 2 + k // 2) * nc, nc)
                for n, piece in enumerate((high_re, high_im, low_re, low_im, high_re, high_im)):
                    left[q, to, n * sd : (n + 1) * sd] = piece
            both = dot(left[q], second[...])
            x_re, x_im = both[: 2 * nc, :sd], both[: 2 * nc, sd:]
            g_re, g_im = both[2 * nc :, :sd], both[2 * nc :, sd:]
            re = x_re * g_re + x_im * g_im
            im = x_re * g_im - x_im * g_re
            total_re = total_re + re[:nc] + re[nc:]
            total_im = total_im + im[:nc] + im[nc:]
        return total_re, total_im

    for n, dy in enumerate(reversed(odd)):
        wait_chip(s4, r4, send4, recv4.at[n]).wait_recv()
        block = r4[:, pl.ds(y_at(dy), 1)].reshape(qs * 2 * zs, sd)
        blocks[pl.ds(y_at(dy), 1)] = dot(moves[4], block).astype(BF16).reshape(1, xs * 2, run, sd)
    for d in range(1, yls):
        spec[:, :sd], spec[:, sd:] = transform(lax.rem(yl + d, yls))
    for dy in reversed(even):
        wait_plane(s2, r2, zs if dy else zs - 1, send2, recv2.at[y_at(dy)]).wait_recv()
        block = r2[pl.ds(y_at(dy) * zs, zs)].reshape(zs * qs * 2, sd)
        blocks[pl.ds(y_at(dy), 1)] = dot(moves[1], block).astype(BF16).reshape(1, xs * 2, run, sd)
    spec_re, spec_im = transform(yl)
    spec_re, spec_im = spec_re + spec[:, :sd], spec_im + spec[:, sd:]

    re_h, re_l = split(spec_re)
    im_h, im_l = split(-spec_im)
    both = dot(jnp.concatenate([re_h, im_h, re_l, im_l, re_h, im_h], axis=1), second[...])
    re, im = both[:, :sd], -both[:, sd:]
    high, low = split(
        jnp.concatenate([re * turn_c - im * turn_s, im * turn_c + re * turn_s], axis=0)
    )
    scale = 2.0 / (2 * nc * sd) / math.sqrt(nc * sd * nh)
    result = dot(last[...], jnp.concatenate([high, low, high], axis=0)) * scale
    for d in range(nc):
        t_own[d] = result[d : d + 1]
    send_to_ctx(t_own, t_all, send_t, recv_t)

    wait_ctx(st_own, st_all, send_s, recv_s).wait_recv()

    def outside(blk, _):
        at = columns(blk)
        rate = rate_ref[:, at]
        weight = ww[:, at]
        fine = []
        for n in range(modes):
            carried = weight[n : n + 1] * st_all[n * nblk + blk]
            eb[n] = carried * jnp.exp(-rate[n : n + 1] * (float(sd - 8) - octs))
            fine.append(jnp.exp(-rate[n : n + 1] * (8.0 - eight)))
        for t in range(tiles):
            total = y[8 * t : 8 * t + 8, at]
            for n in range(modes):
                total = total + jnp.broadcast_to(eb[n, t : t + 1], (8, cb)) * fine[n]
            y[8 * t : 8 * t + 8, at] = total
        return 0

    lax.fori_loop(0, nblk, outside, 0)

    leave = pltpu.make_async_copy(y, y_ref, y_sem)
    leave.start()

    wait_ctx(t_own, t_all, send_t, recv_t).wait_recv()
    gathered = jnp.concatenate([t_all[d] for d in range(nc)], axis=0)
    out_ref[...] = gathered

    leave.wait()
    for source, target, send in ((s1, r1, send1), (s4, r4, send4)):
        some = (pl.ds(0, qs - 1), pl.ds(0, len(even)))
        copy(some_chip, source.at[some], target.at[some], send, recv1.at[0]).wait_send()
    wait_plane(s2, r2, len(even) * zs - 1, send2, recv2.at[0]).wait_send()
    wait_plane(s3, r3, len(odd) * zs, send3, recv3.at[0]).wait_send()
    wait_ctx(u_own, u_all, send_u, recv_u).wait_send()
    wait_ctx(st_own, st_all, send_s, recv_s).wait_send()
    wait_ctx(t_own, t_all, send_t, recv_t).wait_send()


def finish(input_in, filter_in, input_out, filter_out):
    input_out[...] = input_in[...]
    filter_out[...] = filter_in[...]


def body(nc, nh, inputs, out_grad, decay_rate, residue, skip_gain):
    sd, cols = inputs.shape
    modes = decay_rate.shape[0]
    cb = modes * cols // nc
    args = (inputs, out_grad, decay_rate, residue, skip_gain.reshape(1, cols))
    args += tuple(jnp.asarray(t) for t in tables(nc, nh, sd))
    yhs, zs, cores, yls, xs = shape_of(nc, nh)
    ys, qs = yhs * yls, cores * xs
    vmem = pl.BlockSpec(memory_space=pltpu.VMEM)
    dma = pltpu.SemaphoreType.DMA
    input_grad, filter_grad = pl.pallas_call(
        functools.partial(kernel, nc, nh, modes),
        out_shape=(
            jax.ShapeDtypeStruct((sd, cols), F32),
            jax.ShapeDtypeStruct((nc, sd), F32),
        ),
        in_specs=[pl.BlockSpec(memory_space=pltpu.HBM)] * len(args),
        out_specs=(pl.BlockSpec(memory_space=pltpu.HBM), vmem),
        scratch_shapes=[pltpu.VMEM(arg.shape, arg.dtype) for arg in args]
        + [
            pltpu.VMEM((2, cols // (zs * cores), zs * cores, sd), BF16),
            pltpu.VMEM((qs, ys, 2 * zs, sd), BF16),
            pltpu.VMEM((qs, ys, 2 * zs, sd), BF16),
            pltpu.VMEM((ys * zs, qs * 2, sd), BF16),
            pltpu.VMEM((ys * zs, qs * 2, sd), BF16),
            pltpu.VMEM((ys * zs, qs * 2, sd), BF16),
            pltpu.VMEM((ys * zs, qs * 2, sd), BF16),
            pltpu.VMEM((qs, ys, 2 * zs, sd), BF16),
            pltpu.VMEM((qs, ys, 2 * zs, sd), BF16),
            pltpu.VMEM((nc, 1, cb), F32),
            pltpu.VMEM((nc, 1, cb), F32),
            pltpu.VMEM((nc, 1, cb), F32),
            pltpu.VMEM((nc, 1, cb), F32),
            pltpu.VMEM((nc, 1, sd), F32),
            pltpu.VMEM((nc, 1, sd), F32),
            pltpu.VMEM((sd, cols), F32),
            pltpu.VMEM((sd, cols), F32),
            pltpu.VMEM((sd, cols), F32),
            pltpu.VMEM((modes, sd // 8, cb), F32),
            pltpu.VMEM((modes, cols), F32),
            pltpu.VMEM((nc, 1, cb), F32),
            pltpu.VMEM((ys, xs * 2, zs * cores, sd), BF16),
            pltpu.VMEM((xs // 2, 4 * nc, 6 * sd), BF16),
            pltpu.VMEM((nc, 2 * sd), F32),
            dma((len(args),)),
            dma((ys,)),
            dma((ys,)),
            dma((ys,)),
            dma((ys,)),
        ]
        + [dma] * 11,
        compiler_params=pltpu.CompilerParams(
            collective_id=0, has_side_effects=True, vmem_limit_bytes=64 * 1024 * 1024
        ),
        name="modal_backward",
    )(*args)
    input_grad, filter_grad = pl.pallas_call(
        finish,
        out_shape=(jax.ShapeDtypeStruct((sd, cols), F32), jax.ShapeDtypeStruct((nc, sd), F32)),
        in_specs=[vmem, vmem],
        out_specs=(vmem, vmem),
        compiler_params=pltpu.CompilerParams(vmem_limit_bytes=64 * 1024 * 1024),
        name="finish",
    )(input_grad, filter_grad)
    return input_grad, filter_grad.T


def solution(mesh):
    placed = (P("ctx", "ch"), P("ctx", "ch"), P(), P(), P("ch"))
    return jax.shard_map(
        functools.partial(body, mesh.shape["ctx"], mesh.shape["ch"]),
        mesh=mesh,
        in_specs=placed,
        out_specs=(P("ctx", "ch"), P("ctx", "ch")),
        check_vma=False,
    )
```

```python
import functools
import math

import jax
import jax.numpy as jnp
import ml_dtypes
import numpy as np
from jax import lax
from jax.experimental import pallas as pl
from jax.experimental.pallas import tpu as pltpu
from jax.sharding import PartitionSpec as P

MESH = pl.DeviceIdType.MESH
F32 = jnp.float32
BF16 = jnp.bfloat16


def shape_of(nc, nh):
    z = nc // 8 if nc >= 32 else nc // 4
    x = nh // 2
    return nc // (2 * z), z, 2, nh // x, x


def halves(table):
    high = table.astype(np.float32).astype(ml_dtypes.bfloat16)
    low = (table - high.astype(np.float64)).astype(np.float32).astype(ml_dtypes.bfloat16)
    return high, low


def reorder(sizes, old, new):
    count = np.arange(math.prod(sizes[axis] for axis in old)).reshape([sizes[axis] for axis in old])
    moved = count.transpose([old.index(axis) for axis in new]).reshape(-1)
    return np.eye(moved.size, dtype=np.float32)[moved]


@functools.lru_cache(maxsize=None)
def tables(nc, nh, sd):
    _, zs, cores, _, xs = shape_of(nc, nh)
    j = np.arange(nc) + 0.5
    a = np.arange(nc)
    s = np.arange(sd)
    full = 2 * nc * sd
    angle = 2.0 * np.pi * np.outer(j, a) / (2 * nc)
    block = np.concatenate([np.cos(angle), -np.sin(angle)], axis=0)
    high, low = halves(block)
    first = np.concatenate([high, low], axis=1)
    last_h, last_l = halves(block.T.copy())
    last = np.concatenate([last_h, last_h, last_l], axis=1)
    angle = 2.0 * np.pi * np.outer(j, s) / full
    twist = np.stack([np.cos(angle), np.sin(angle)]).astype(np.float32)
    angle = 2.0 * np.pi * (np.outer(s, s) % sd) / sd
    cos, sin = np.cos(angle), np.sin(angle)
    step = np.concatenate([np.concatenate([cos, -sin], axis=1), np.concatenate([sin, cos], axis=1)], axis=0)
    high, low = halves(step)
    second = np.concatenate([high, high, low], axis=0)
    angle = 2.0 * np.pi * np.outer(s + 0.5, s) / (2 * sd)
    near = np.concatenate([np.cos(angle), -np.sin(angle)], axis=0)
    high, low = halves(near)
    near_in = np.concatenate([high, low, high], axis=1)
    near_out = np.concatenate([high.T, high.T, low.T], axis=1)
    qx = {"q": cores * xs, "core": cores, "x": xs, "arr": 2, "z": zs}
    moves = [
        reorder(qx, ("core", "x", "arr", "z"), ("z", "core", "x", "arr")),
        reorder(qx, ("z", "core", "x", "arr"), ("x", "arr", "z", "core")),
        reorder(qx, ("arr", "x", "core", "z"), ("z", "arr", "core", "x")),
        reorder(qx, ("z", "arr", "core", "x"), ("core", "x", "arr", "z")),
        reorder(qx, ("core", "x", "arr", "z"), ("x", "arr", "z", "core")),
    ]
    bf = ml_dtypes.bfloat16
    return (
        np.stack(moves).astype(bf),
        first,
        np.ascontiguousarray(second),
        last,
        twist,
        near_in,
        np.ascontiguousarray(near_out),
    )


def split(value):
    high = value.astype(BF16)
    return high, (value - high.astype(F32)).astype(BF16)


def dot(left, right):
    return jnp.dot(left, right, preferred_element_type=F32)


def kernel(nc, nh, modes, *refs):
    args_in, refs = refs[:12], refs[12:]
    (y_ref, out_ref), refs = refs[:2], refs[2:]
    args, refs = refs[:12], refs[12:]
    x_ref, g_ref, rate_ref, res_ref, gain_ref, moves, first, second, last, twist, near_in, near_out = args
    (runs, s1, r1, s2, r2, s3, r3, s4, r4), refs = refs[:9], refs[9:]
    (u_own, u_all, st_own, st_all, t_own, t_all), refs = refs[:6], refs[6:]
    (y, grad, taps, eb, ww, rate_rows, blocks, left, spec), refs = refs[:9], refs[9:]
    (table_sem, recv1, recv2, recv3, recv4, y_sem, send1, send2, send3, send4, send_u, recv_u, send_s, recv_s, send_t, recv_t) = refs

    sd, cols = x_ref.shape
    cb = modes * cols // nc
    nblk = cols // cb
    tiles = sd // 8
    yhs, zs, cores, yls, xs = shape_of(nc, nh)
    ys, qs, run = yhs * yls, cores * xs, zs * cores
    me = lax.axis_index("ctx")
    my = lax.axis_index("ch")
    yh, z, core = me // run, lax.rem(me, run) // cores, lax.rem(me, cores)
    yl, x = my // xs, lax.rem(my, xs)
    y_me = yh * yls + yl
    q_me = core * xs + x

    def farthest(count):
        return sorted(range(count), key=lambda d: -min(d, count - d))

    far_y = farthest(ys)
    even = [dy for dy in far_y if dy % yls == 0]
    odd = [dy for dy in far_y if dy % yls]
    q_steps = [(dc, dx) for dx in farthest(xs) for dc in (1, 0)][:-1]

    def z_at(m):
        return lax.rem(z + zs // 2 + ((m + 1) // 2) * (2 * lax.rem(m, 2) - 1) + zs, zs)

    def y_at(dy):
        return lax.rem(y_me + dy, ys)

    def plane_peer(dy, m):
        there = y_at(dy)
        device = {"ctx": (there // yls * zs + z_at(m)) * cores + core, "ch": lax.rem(there, yls) * xs + x}
        return device, there * zs + z_at(m)

    def chip_peer(step):
        dc, dx = step
        core_at, x_at = lax.rem(core + dc, cores), lax.rem(x + dx, xs)
        return {"ctx": me - core + core_at, "ch": yl * xs + x_at}, core_at * xs + x_at

    def ctx_peer(dyh, t):
        return (lax.rem(yh + dyh, yhs) * zs + z_at(t // cores)) * cores + lax.rem(core + 1 - lax.rem(t, cores), cores)

    def each_plane(dy, act):
        def body(m, _):
            act(*plane_peer(dy, m))
            return 0

        lax.fori_loop(0, zs if dy else zs - 1, body, 0)

    def each_ctx(dyh, act):
        def body(t, _):
            act(ctx_peer(dyh, t))
            return 0

        lax.fori_loop(0, run if dyh else run - 1, body, 0)

    barrier = pltpu.get_barrier_semaphore()

    def greet(device, _):
        pl.semaphore_signal(barrier, inc=1, device_id=device, device_id_type=MESH)

    loads = [
        pltpu.make_async_copy(src, dst, table_sem.at[n]) for n, (src, dst) in enumerate(zip(args_in, args))
    ]
    for load in loads[:5]:
        load.start()

    for n, dy in enumerate(far_y):
        each_plane(dy, greet)
        if n == 2:
            for step in q_steps:
                greet(*chip_peer(step))

    for dyh in farthest(yhs):
        def other(m, _):
            device = (lax.rem(yh + dyh, yhs) * zs + z_at(m)) * cores + lax.rem(core + 1, cores)
            greet({"ctx": device}, 0)
            return 0

        lax.fori_loop(0, zs if dyh else zs - 1, other, 0)

    for load in loads[5:]:
        load.start()

    width = min(cols, 256)
    row = lax.broadcasted_iota(jnp.int32, (width, width), 0)
    turn = (
        (row & -run) + (row & (zs - 1)) * cores + ((row & (run - 1)) // zs)
        == lax.broadcasted_iota(jnp.int32, (width, width), 1)
    ).astype(F32).astype(BF16)
    loads[0].wait()
    loads[1].wait()
    for c0 in range(0, cols, width):
        pair_of = [
            lax.dot_general(turn, ref[:, c0 : c0 + width], (((1,), (1,)), ((), ())), preferred_element_type=F32)
            for ref in (x_ref, g_ref)
        ]
        for r0 in range(0, width, zs):
            c = c0 + r0
            to_core = c % run // zs
            to_yh = c // run % yhs
            to_yl, to_x = c // nc // xs, c // nc % xs
            both = jnp.concatenate([part[r0 : r0 + zs] for part in pair_of], axis=0)
            s1[to_core * xs + to_x, to_yh * yls + to_yl] = both.astype(BF16)
        for r0 in range(0, width, run):
            for arr in range(2):
                runs[arr, (c0 + r0) // run] = pair_of[arr][r0 : r0 + run].astype(BF16)
    def copy(device, src, dst, send, recv):
        return pltpu.make_async_remote_copy(
            src_ref=src, dst_ref=dst, send_sem=send, recv_sem=recv, device_id=device, device_id_type=MESH
        )

    some_chip, _ = chip_peer(q_steps[0])
    some_plane, _ = plane_peer(far_y[0], 0)
    def ctx_copy(peer, src, dst, send, recv):
        return copy({"ctx": peer}, src, dst, send, recv)

    def send_to_ctx(own, everyone, send, recv):
        for dyh in farthest(yhs):
            each_ctx(dyh, lambda peer: ctx_copy(peer, own.at[peer], everyone.at[me], send, recv).start())
        everyone[pl.ds(me, 1)] = own[pl.ds(me, 1)]

    def wait_ctx(own, everyone, send, recv, count=nc - 1):
        return ctx_copy(ctx_peer(0, 0), own.at[pl.ds(0, count)], everyone.at[pl.ds(0, count)], send, recv)

    pl.semaphore_wait(barrier, (ys * zs - 1) + (qs - 1) + (yhs * zs - 1))

    def to_chip(source, target, y, send, recv):
        for step in q_steps:
            device, q_at = chip_peer(step)
            copy(device, source.at[q_at, y], target.at[q_me, y], send, recv).start()
        target[pl.ds(q_me, 1), pl.ds(y, 1)] = source[pl.ds(q_me, 1), pl.ds(y, 1)]

    def to_plane(source, target, dy, send, recv):
        def onward(device, at):
            copy(device, source.at[at], target.at[y_me * zs + z], send, recv).start()

        each_plane(dy, onward)

    def wait_chip(source, target, send, recv):
        return copy(some_chip, source.at[pl.ds(0, qs - 1), 0], target.at[pl.ds(0, qs - 1), 0], send, recv)

    def wait_plane(source, target, count, send, recv):
        return copy(some_plane, source.at[pl.ds(0, count)], target.at[pl.ds(0, count)], send, recv)

    for n, dy in enumerate(even):
        to_chip(s1, r1, y_at(dy), send1, recv1.at[n])
    loads[5].wait()
    for dy in odd:
        there = y_at(dy)
        first_run = lax.rem(there, yls) * xs * yhs + there // yls
        piece = [runs[arr, first_run + to_x * yhs] for arr in range(2) for to_x in range(xs)]
        piece = dot(moves[2], jnp.concatenate(piece, axis=0))
        s3[pl.ds(there * zs, zs)] = piece.astype(BF16).reshape(zs, qs * 2, sd)
        to_plane(s3, r3, dy, send3, recv3.at[y_me])

    for n in (2, 3, 4):
        loads[n].wait()

    grad[...] = g_ref[...].astype(F32)
    eight = lax.broadcasted_iota(jnp.int32, (8, cb), 0).astype(F32)
    octs = 8.0 * lax.broadcasted_iota(jnp.int32, (tiles, cb), 0).astype(F32)

    def weight_of(rate, residue):
        x = 2.0 * rate
        series = 1.0 - x * (1.0 / 7.0)
        for n in (6, 5, 4, 3, 2):
            series = 1.0 - (x * (1.0 / n)) * series
        return residue * jnp.sqrt(x * series)

    def columns(blk):
        return pl.ds(pl.multiple_of(blk * cb, cb), cb)

    def states(blk, _):
        at = columns(blk)
        rate = rate_ref[:, at]
        weight = weight_of(rate, res_ref[:, at])
        ww[:, at] = weight
        for n in range(modes):
            slow = jnp.exp(-rate[n : n + 1] * octs)
            eb[n] = slow
        fine = [jnp.exp(-rate[n : n + 1] * eight) for n in range(modes)]
        scaled = [fine[n] * weight[n : n + 1] for n in range(modes)]
        sums = [jnp.zeros((8, cb), F32) for _ in range(modes)]
        for t in range(tiles):
            g = grad[8 * t : 8 * t + 8, at]
            tap = jnp.zeros((8, cb), F32)
            for n in range(modes):
                level = jnp.broadcast_to(eb[n, t : t + 1], (8, cb))
                sums[n] = sums[n] + level * g
                tap = tap + level * scaled[n]
            taps[8 * t : 8 * t + 8, at] = tap
        for n in range(modes):
            rate_rows[n * nblk + blk] = rate[n : n + 1]
            u_own[n * nblk + blk] = jnp.sum(sums[n] * fine[n], axis=0, keepdims=True)
        return 0

    lax.fori_loop(0, nblk, states, 0)

    send_to_ctx(u_own, u_all, send_u, recv_u)

    for n, dy in enumerate(even):
        wait_chip(s1, r1, send1, recv1.at[n]).wait_recv()
        block = r1[:, pl.ds(y_at(dy), 1)].reshape(qs * 2 * zs, sd)
        s2[pl.ds(y_at(dy) * zs, zs)] = dot(moves[0], block).astype(BF16).reshape(zs, qs * 2, sd)
        to_plane(s2, r2, dy, send2, recv2.at[y_me])
    own = pl.ds(y_me * zs + z, 1)
    r2[own] = s2[own]

    loads[10].wait()
    loads[11].wait()
    wide = min(cols, 256)

    def inside(blk, _):
        at = pl.ds(pl.multiple_of(blk * wide, wide), wide)
        g = g_ref[:, at]
        g_spec = dot(near_in[:, : 2 * sd], jnp.concatenate([g, g], axis=0))
        high, low = split(taps[:, at])
        h_spec = dot(near_in[...], jnp.concatenate([high, high, low], axis=0))
        g_re, g_im = g_spec[:sd], g_spec[sd:]
        h_re, h_im = h_spec[:sd], h_spec[sd:]
        term = jnp.concatenate([h_re * g_re + h_im * g_im, h_re * g_im - h_im * g_re], axis=0)
        high, low = split(term)
        part = dot(near_out[...], jnp.concatenate([high, low, high], axis=0)) * (1.0 / sd)
        y[:, at] = part + gain_ref[:, at] * grad[:, at]
        return 0

    lax.fori_loop(0, cols // wide, inside, 0)

    for n, dy in enumerate(reversed(odd)):
        wait_plane(s3, r3, zs, send3, recv3.at[y_at(dy)]).wait_recv()
        block = r3[pl.ds(y_at(dy) * zs, zs)].reshape(zs * qs * 2, sd)
        s4[:, pl.ds(y_at(dy), 1)] = dot(moves[3], block).astype(BF16).reshape(qs, 1, 2 * zs, sd)
        to_chip(s4, r4, y_at(dy), send4, recv4.at[n])

    wait_ctx(u_own, u_all, send_u, recv_u).wait_recv()
    decay = jnp.exp(-rate_rows[me] * float(sd))
    state = jnp.zeros((1, cb), F32)
    for p in range(nc - 1, -1, -1):
        st_own[p] = state
        state = u_all[p] + decay * state
    send_to_ctx(st_own, st_all, send_s, recv_s)

    for n in (6, 7, 8, 9):
        loads[n].wait()
    turn_c, turn_s = twist[0], twist[1]

    def transform(part_of_y):
        total_re, total_im = 0.0, 0.0
        for q in range(xs // 2):
            for k in range(4):
                at = (2 * q + k // 2) * 2 + k % 2
                part = [blocks[a * yls + part_of_y, at] for a in range(yhs)]
                freq = dot(first[...], jnp.concatenate(part + part, axis=0))
                re, im = freq[:nc], freq[nc:]
                high_re, low_re = split(re * turn_c + im * turn_s)
                high_im, low_im = split(im * turn_c - re * turn_s)
                to = pl.ds(((k % 2) * 2 + k // 2) * nc, nc)
                for n, piece in enumerate((high_re, high_im, low_re, low_im, high_re, high_im)):
                    left[q, to, n * sd : (n + 1) * sd] = piece
            both = dot(left[q], second[...])
            x_re, x_im = both[: 2 * nc, :sd], both[: 2 * nc, sd:]
            g_re, g_im = both[2 * nc :, :sd], both[2 * nc :, sd:]
            re = x_re * g_re + x_im * g_im
            im = x_re * g_im - x_im * g_re
            total_re = total_re + re[:nc] + re[nc:]
            total_im = total_im + im[:nc] + im[nc:]
        return total_re, total_im

    for n, dy in enumerate(reversed(odd)):
        wait_chip(s4, r4, send4, recv4.at[n]).wait_recv()
        block = r4[:, pl.ds(y_at(dy), 1)].reshape(qs * 2 * zs, sd)
        blocks[pl.ds(y_at(dy), 1)] = dot(moves[4], block).astype(BF16).reshape(1, xs * 2, run, sd)
    for d in range(1, yls):
        spec[:, :sd], spec[:, sd:] = transform(lax.rem(yl + d, yls))
    for dy in reversed(even):
        wait_plane(s2, r2, zs if dy else zs - 1, send2, recv2.at[y_at(dy)]).wait_recv()
        block = r2[pl.ds(y_at(dy) * zs, zs)].reshape(zs * qs * 2, sd)
        blocks[pl.ds(y_at(dy), 1)] = dot(moves[1], block).astype(BF16).reshape(1, xs * 2, run, sd)
    spec_re, spec_im = transform(yl)
    spec_re, spec_im = spec_re + spec[:, :sd], spec_im + spec[:, sd:]

    re_h, re_l = split(spec_re)
    im_h, im_l = split(-spec_im)
    both = dot(jnp.concatenate([re_h, im_h, re_l, im_l, re_h, im_h], axis=1), second[...])
    re, im = both[:, :sd], -both[:, sd:]
    high, low = split(
        jnp.concatenate([re * turn_c - im * turn_s, im * turn_c + re * turn_s], axis=0)
    )
    scale = 2.0 / (2 * nc * sd) / math.sqrt(nc * sd * nh)
    result = dot(last[...], jnp.concatenate([high, low, high], axis=0)) * scale
    for d in range(nc):
        t_own[d] = result[d : d + 1]
    send_to_ctx(t_own, t_all, send_t, recv_t)

    wait_ctx(st_own, st_all, send_s, recv_s).wait_recv()

    def outside(blk, _):
        at = columns(blk)
        rate = rate_ref[:, at]
        weight = ww[:, at]
        fine = []
        for n in range(modes):
            carried = weight[n : n + 1] * st_all[n * nblk + blk]
            eb[n] = carried * jnp.exp(-rate[n : n + 1] * (float(sd - 8) - octs))
            fine.append(jnp.exp(-rate[n : n + 1] * (8.0 - eight)))
        for t in range(tiles):
            total = y[8 * t : 8 * t + 8, at]
            for n in range(modes):
                total = total + jnp.broadcast_to(eb[n, t : t + 1], (8, cb)) * fine[n]
            y[8 * t : 8 * t + 8, at] = total
        return 0

    lax.fori_loop(0, nblk, outside, 0)

    leave = pltpu.make_async_copy(y, y_ref, y_sem)
    leave.start()

    wait_ctx(t_own, t_all, send_t, recv_t).wait_recv()
    gathered = jnp.concatenate([t_all[d] for d in range(nc)], axis=0)
    out_ref[...] = gathered

    leave.wait()
    for source, target, send in ((s1, r1, send1), (s4, r4, send4)):
        some = (pl.ds(0, qs - 1), pl.ds(0, len(even)))
        copy(some_chip, source.at[some], target.at[some], send, recv1.at[0]).wait_send()
    wait_plane(s2, r2, len(even) * zs - 1, send2, recv2.at[0]).wait_send()
    wait_plane(s3, r3, len(odd) * zs, send3, recv3.at[0]).wait_send()
    wait_ctx(u_own, u_all, send_u, recv_u).wait_send()
    wait_ctx(st_own, st_all, send_s, recv_s).wait_send()
    wait_ctx(t_own, t_all, send_t, recv_t).wait_send()


def finish(input_in, filter_in, input_out, filter_out):
    input_out[...] = input_in[...]
    filter_out[...] = filter_in[...]


def body(nc, nh, inputs, out_grad, decay_rate, residue, skip_gain):
    sd, cols = inputs.shape
    modes = decay_rate.shape[0]
    cb = modes * cols // nc
    args = (inputs, out_grad, decay_rate, residue, skip_gain.reshape(1, cols))
    args += tuple(jnp.asarray(t) for t in tables(nc, nh, sd))
    yhs, zs, cores, yls, xs = shape_of(nc, nh)
    ys, qs = yhs * yls, cores * xs
    vmem = pl.BlockSpec(memory_space=pltpu.VMEM)
    dma = pltpu.SemaphoreType.DMA
    input_grad, filter_grad = pl.pallas_call(
        functools.partial(kernel, nc, nh, modes),
        out_shape=(
            jax.ShapeDtypeStruct((sd, cols), F32),
            jax.ShapeDtypeStruct((nc, sd), F32),
        ),
        in_specs=[pl.BlockSpec(memory_space=pltpu.HBM)] * len(args),
        out_specs=(pl.BlockSpec(memory_space=pltpu.HBM), vmem),
        scratch_shapes=[pltpu.VMEM(arg.shape, arg.dtype) for arg in args]
        + [
            pltpu.VMEM((2, cols // (zs * cores), zs * cores, sd), BF16),
            pltpu.VMEM((qs, ys, 2 * zs, sd), BF16),
            pltpu.VMEM((qs, ys, 2 * zs, sd), BF16),
            pltpu.VMEM((ys * zs, qs * 2, sd), BF16),
            pltpu.VMEM((ys * zs, qs * 2, sd), BF16),
            pltpu.VMEM((ys * zs, qs * 2, sd), BF16),
            pltpu.VMEM((ys * zs, qs * 2, sd), BF16),
            pltpu.VMEM((qs, ys, 2 * zs, sd), BF16),
            pltpu.VMEM((qs, ys, 2 * zs, sd), BF16),
            pltpu.VMEM((nc, 1, cb), F32),
            pltpu.VMEM((nc, 1, cb), F32),
            pltpu.VMEM((nc, 1, cb), F32),
            pltpu.VMEM((nc, 1, cb), F32),
            pltpu.VMEM((nc, 1, sd), F32),
            pltpu.VMEM((nc, 1, sd), F32),
            pltpu.VMEM((sd, cols), F32),
            pltpu.VMEM((sd, cols), F32),
            pltpu.VMEM((sd, cols), F32),
            pltpu.VMEM((modes, sd // 8, cb), F32),
            pltpu.VMEM((modes, cols), F32),
            pltpu.VMEM((nc, 1, cb), F32),
            pltpu.VMEM((ys, xs * 2, zs * cores, sd), BF16),
            pltpu.VMEM((xs // 2, 4 * nc, 6 * sd), BF16),
            pltpu.VMEM((nc, 2 * sd), F32),
            dma((len(args),)),
            dma((ys,)),
            dma((ys,)),
            dma((ys,)),
            dma((ys,)),
        ]
        + [dma] * 11,
        compiler_params=pltpu.CompilerParams(
            collective_id=0, has_side_effects=True, vmem_limit_bytes=64 * 1024 * 1024
        ),
        name="modal_backward",
    )(*args)
    input_grad, filter_grad = pl.pallas_call(
        finish,
        out_shape=(jax.ShapeDtypeStruct((sd, cols), F32), jax.ShapeDtypeStruct((nc, sd), F32)),
        in_specs=[vmem, vmem],
        out_specs=(vmem, vmem),
        compiler_params=pltpu.CompilerParams(vmem_limit_bytes=64 * 1024 * 1024),
        name="finish",
    )(input_grad, filter_grad)
    return input_grad, filter_grad.T


def solution(mesh):
    placed = (P("ctx", "ch"), P("ctx", "ch"), P(), P(), P("ch"))
    return jax.shard_map(
        functools.partial(body, mesh.shape["ctx"], mesh.shape["ch"]),
        mesh=mesh,
        in_specs=placed,
        out_specs=(P("ctx", "ch"), P("ctx", "ch")),
        check_vma=False,
    )
```

```python
import functools
import math

import jax
import jax.numpy as jnp
import ml_dtypes
import numpy as np
from jax import lax
from jax.experimental import pallas as pl
from jax.experimental.pallas import tpu as pltpu
from jax.sharding import PartitionSpec as P

MESH = pl.DeviceIdType.MESH
F32 = jnp.float32
BF16 = jnp.bfloat16


def shape_of(nc, nh):
    z = nc // 8 if nc >= 32 else nc // 4
    x = nh // 2
    return nc // (2 * z), z, 2, nh // x, x


def halves(table):
    high = table.astype(np.float32).astype(ml_dtypes.bfloat16)
    low = (table - high.astype(np.float64)).astype(np.float32).astype(ml_dtypes.bfloat16)
    return high, low


def reorder(sizes, old, new):
    count = np.arange(math.prod(sizes[axis] for axis in old)).reshape([sizes[axis] for axis in old])
    moved = count.transpose([old.index(axis) for axis in new]).reshape(-1)
    return np.eye(moved.size, dtype=np.float32)[moved]


@functools.lru_cache(maxsize=None)
def tables(nc, nh, sd):
    _, zs, cores, _, xs = shape_of(nc, nh)
    j = np.arange(nc) + 0.5
    a = np.arange(nc)
    s = np.arange(sd)
    full = 2 * nc * sd
    angle = 2.0 * np.pi * np.outer(j, a) / (2 * nc)
    block = np.concatenate([np.cos(angle), -np.sin(angle)], axis=0)
    high, low = halves(block)
    first = np.concatenate([high, low], axis=1)
    last_h, last_l = halves(block.T.copy())
    last = np.concatenate([last_h, last_h, last_l], axis=1)
    angle = 2.0 * np.pi * np.outer(j, s) / full
    twist = np.stack([np.cos(angle), np.sin(angle)]).astype(np.float32)
    angle = 2.0 * np.pi * (np.outer(s, s) % sd) / sd
    cos, sin = np.cos(angle), np.sin(angle)
    step = np.concatenate([np.concatenate([cos, -sin], axis=1), np.concatenate([sin, cos], axis=1)], axis=0)
    high, low = halves(step)
    second = np.concatenate([high, high, low], axis=0)
    angle = 2.0 * np.pi * np.outer(s + 0.5, s) / (2 * sd)
    near = np.concatenate([np.cos(angle), -np.sin(angle)], axis=0)
    high, low = halves(near)
    near_in = np.concatenate([high, low, high], axis=1)
    near_out = np.concatenate([high.T, high.T, low.T], axis=1)
    qx = {"q": cores * xs, "core": cores, "x": xs, "arr": 2, "z": zs}
    moves = [
        reorder(qx, ("core", "x", "arr", "z"), ("z", "core", "x", "arr")),
        reorder(qx, ("z", "core", "x", "arr"), ("x", "arr", "z", "core")),
        reorder(qx, ("arr", "x", "core", "z"), ("z", "arr", "core", "x")),
        reorder(qx, ("z", "arr", "core", "x"), ("core", "x", "arr", "z")),
        reorder(qx, ("core", "x", "arr", "z"), ("x", "arr", "z", "core")),
    ]
    bf = ml_dtypes.bfloat16
    return (
        np.stack(moves).astype(bf),
        first,
        np.ascontiguousarray(second),
        last,
        twist,
        near_in,
        np.ascontiguousarray(near_out),
    )


def split(value):
    high = value.astype(BF16)
    return high, (value - high.astype(F32)).astype(BF16)


def dot(left, right):
    return jnp.dot(left, right, preferred_element_type=F32)


def kernel(nc, nh, modes, *refs):
    args_in, refs = refs[:12], refs[12:]
    (y_ref, out_ref), refs = refs[:2], refs[2:]
    args, refs = refs[:12], refs[12:]
    x_ref, g_ref, rate_ref, res_ref, gain_ref, moves, first, second, last, twist, near_in, near_out = args
    (runs, s1, r1, s2, r2, s3, r3, s4, r4), refs = refs[:9], refs[9:]
    (u_own, u_all, st_own, st_all, t_own, t_all), refs = refs[:6], refs[6:]
    (y, grad, taps, eb, ww, rate_rows, blocks, left, spec), refs = refs[:9], refs[9:]
    (table_sem, recv1, recv2, recv3, recv4, y_sem, send1, send2, send3, send4, send_u, recv_u, send_s, recv_s, send_t, recv_t) = refs

    sd, cols = x_ref.shape
    cb = modes * cols // nc
    nblk = cols // cb
    tiles = sd // 8
    yhs, zs, cores, yls, xs = shape_of(nc, nh)
    ys, qs, run = yhs * yls, cores * xs, zs * cores
    me = lax.axis_index("ctx")
    my = lax.axis_index("ch")
    yh, z, core = me // run, lax.rem(me, run) // cores, lax.rem(me, cores)
    yl, x = my // xs, lax.rem(my, xs)
    y_me = yh * yls + yl
    q_me = core * xs + x

    def farthest(count):
        return sorted(range(count), key=lambda d: -min(d, count - d))

    far_y = farthest(ys)
    even = [dy for dy in far_y if dy % yls == 0]
    odd = [dy for dy in far_y if dy % yls]
    q_steps = [(dc, dx) for dx in farthest(xs) for dc in (1, 0)][:-1]

    def z_at(m):
        return lax.rem(z + zs // 2 + ((m + 1) // 2) * (2 * lax.rem(m, 2) - 1) + zs, zs)

    def y_at(dy):
        return lax.rem(y_me + dy, ys)

    def plane_peer(dy, m):
        there = y_at(dy)
        device = {"ctx": (there // yls * zs + z_at(m)) * cores + core, "ch": lax.rem(there, yls) * xs + x}
        return device, there * zs + z_at(m)

    def chip_peer(step):
        dc, dx = step
        core_at, x_at = lax.rem(core + dc, cores), lax.rem(x + dx, xs)
        return {"ctx": me - core + core_at, "ch": yl * xs + x_at}, core_at * xs + x_at

    def ctx_peer(dyh, t):
        return (lax.rem(yh + dyh, yhs) * zs + z_at(t // cores)) * cores + lax.rem(core + 1 - lax.rem(t, cores), cores)

    def each_plane(dy, act):
        def body(m, _):
            act(*plane_peer(dy, m))
            return 0

        lax.fori_loop(0, zs if dy else zs - 1, body, 0)

    def each_ctx(dyh, act):
        def body(t, _):
            act(ctx_peer(dyh, t))
            return 0

        lax.fori_loop(0, run if dyh else run - 1, body, 0)

    barrier = pltpu.get_barrier_semaphore()

    def greet(device, _):
        pl.semaphore_signal(barrier, inc=1, device_id=device, device_id_type=MESH)

    loads = [
        pltpu.make_async_copy(src, dst, table_sem.at[n]) for n, (src, dst) in enumerate(zip(args_in, args))
    ]
    for load in loads[:5]:
        load.start()

    for n, dy in enumerate(far_y):
        each_plane(dy, greet)
        if n == 2:
            for step in q_steps:
                greet(*chip_peer(step))

    for dyh in farthest(yhs):
        def other(m, _):
            device = (lax.rem(yh + dyh, yhs) * zs + z_at(m)) * cores + lax.rem(core + 1, cores)
            greet({"ctx": device}, 0)
            return 0

        lax.fori_loop(0, zs if dyh else zs - 1, other, 0)

    for load in loads[5:]:
        load.start()

    width = min(cols, 256)
    row = lax.broadcasted_iota(jnp.int32, (width, width), 0)
    turn = (
        (row & -run) + (row & (zs - 1)) * cores + ((row & (run - 1)) // zs)
        == lax.broadcasted_iota(jnp.int32, (width, width), 1)
    ).astype(F32).astype(BF16)
    loads[0].wait()
    loads[1].wait()
    for c0 in range(0, cols, width):
        pair_of = [
            lax.dot_general(turn, ref[:, c0 : c0 + width], (((1,), (1,)), ((), ())), preferred_element_type=F32)
            for ref in (x_ref, g_ref)
        ]
        for r0 in range(0, width, zs):
            c = c0 + r0
            to_core = c % run // zs
            to_yh = c // run % yhs
            to_yl, to_x = c // nc // xs, c // nc % xs
            both = jnp.concatenate([part[r0 : r0 + zs] for part in pair_of], axis=0)
            s1[to_core * xs + to_x, to_yh * yls + to_yl] = both.astype(BF16)
        for r0 in range(0, width, run):
            for arr in range(2):
                runs[arr, (c0 + r0) // run] = pair_of[arr][r0 : r0 + run].astype(BF16)

    def copy(device, src, dst, send, recv):
        return pltpu.make_async_remote_copy(
            src_ref=src, dst_ref=dst, send_sem=send, recv_sem=recv, device_id=device, device_id_type=MESH
        )

    some_chip, _ = chip_peer(q_steps[0])
    some_plane, _ = plane_peer(far_y[0], 0)

    def ctx_copy(peer, src, dst, send, recv):
        return copy({"ctx": peer}, src, dst, send, recv)

    def send_to_ctx(own, everyone, send, recv):
        for dyh in farthest(yhs):
            each_ctx(dyh, lambda peer: ctx_copy(peer, own.at[peer], everyone.at[me], send, recv).start())
        everyone[pl.ds(me, 1)] = own[pl.ds(me, 1)]

    def wait_ctx(own, everyone, send, recv, count=nc - 1):
        return ctx_copy(ctx_peer(0, 0), own.at[pl.ds(0, count)], everyone.at[pl.ds(0, count)], send, recv)

    pl.semaphore_wait(barrier, (ys * zs - 1) + (qs - 1) + (yhs * zs - 1))

    def to_chip(source, target, y, send, recv):
        for step in q_steps:
            device, q_at = chip_peer(step)
            copy(device, source.at[q_at, y], target.at[q_me, y], send, recv).start()
        target[pl.ds(q_me, 1), pl.ds(y, 1)] = source[pl.ds(q_me, 1), pl.ds(y, 1)]

    def to_plane(source, target, dy, send, recv):
        def onward(device, at):
            copy(device, source.at[at], target.at[y_me * zs + z], send, recv).start()

        each_plane(dy, onward)

    def wait_chip(source, target, send, recv):
        return copy(some_chip, source.at[pl.ds(0, qs - 1), 0], target.at[pl.ds(0, qs - 1), 0], send, recv)

    def wait_plane(source, target, count, send, recv):
        return copy(some_plane, source.at[pl.ds(0, count)], target.at[pl.ds(0, count)], send, recv)

    for n, dy in enumerate(even):
        to_chip(s1, r1, y_at(dy), send1, recv1.at[n])
    loads[5].wait()
    for dy in odd:
        there = y_at(dy)
        first_run = lax.rem(there, yls) * xs * yhs + there // yls
        piece = [runs[arr, first_run + to_x * yhs] for arr in range(2) for to_x in range(xs)]
        piece = dot(moves[2], jnp.concatenate(piece, axis=0))
        s3[pl.ds(there * zs, zs)] = piece.astype(BF16).reshape(zs, qs * 2, sd)

    def both_ways(m, _):
        for dy in odd:
            device, at = plane_peer(dy, m)
            copy(device, s3.at[at], r3.at[y_me * zs + z], send3, recv3.at[y_me]).start()
        return 0

    lax.fori_loop(0, zs, both_ways, 0)

    for n in (2, 3, 4):
        loads[n].wait()

    grad[...] = g_ref[...].astype(F32)
    eight = lax.broadcasted_iota(jnp.int32, (8, cb), 0).astype(F32)
    octs = 8.0 * lax.broadcasted_iota(jnp.int32, (tiles, cb), 0).astype(F32)

    def weight_of(rate, residue):
        x = 2.0 * rate
        series = 1.0 - x * (1.0 / 7.0)
        for n in (6, 5, 4, 3, 2):
            series = 1.0 - (x * (1.0 / n)) * series
        return residue * jnp.sqrt(x * series)

    def columns(blk):
        return pl.ds(pl.multiple_of(blk * cb, cb), cb)

    def states(blk, _):
        at = columns(blk)
        rate = rate_ref[:, at]
        weight = weight_of(rate, res_ref[:, at])
        ww[:, at] = weight
        for n in range(modes):
            slow = jnp.exp(-rate[n : n + 1] * octs)
            eb[n] = slow
        fine = [jnp.exp(-rate[n : n + 1] * eight) for n in range(modes)]
        scaled = [fine[n] * weight[n : n + 1] for n in range(modes)]
        sums = [jnp.zeros((8, cb), F32) for _ in range(modes)]
        for t in range(tiles):
            g = grad[8 * t : 8 * t + 8, at]
            tap = jnp.zeros((8, cb), F32)
            for n in range(modes):
                level = jnp.broadcast_to(eb[n, t : t + 1], (8, cb))
                sums[n] = sums[n] + level * g
                tap = tap + level * scaled[n]
            taps[8 * t : 8 * t + 8, at] = tap
        for n in range(modes):
            rate_rows[n * nblk + blk] = rate[n : n + 1]
            u_own[n * nblk + blk] = jnp.sum(sums[n] * fine[n], axis=0, keepdims=True)
        return 0

    lax.fori_loop(0, nblk, states, 0)

    send_to_ctx(u_own, u_all, send_u, recv_u)

    for n, dy in enumerate(even):
        wait_chip(s1, r1, send1, recv1.at[n]).wait_recv()
        block = r1[:, pl.ds(y_at(dy), 1)].reshape(qs * 2 * zs, sd)
        s2[pl.ds(y_at(dy) * zs, zs)] = dot(moves[0], block).astype(BF16).reshape(zs, qs * 2, sd)
        to_plane(s2, r2, dy, send2, recv2.at[y_me])
    own = pl.ds(y_me * zs + z, 1)
    r2[own] = s2[own]

    loads[10].wait()
    loads[11].wait()
    wide = min(cols, 256)

    def inside(blk, _):
        at = pl.ds(pl.multiple_of(blk * wide, wide), wide)
        g = g_ref[:, at]
        g_spec = dot(near_in[:, : 2 * sd], jnp.concatenate([g, g], axis=0))
        high, low = split(taps[:, at])
        h_spec = dot(near_in[...], jnp.concatenate([high, high, low], axis=0))
        g_re, g_im = g_spec[:sd], g_spec[sd:]
        h_re, h_im = h_spec[:sd], h_spec[sd:]
        term = jnp.concatenate([h_re * g_re + h_im * g_im, h_re * g_im - h_im * g_re], axis=0)
        high, low = split(term)
        part = dot(near_out[...], jnp.concatenate([high, low, high], axis=0)) * (1.0 / sd)
        y[:, at] = part + gain_ref[:, at] * grad[:, at]
        return 0

    lax.fori_loop(0, cols // wide, inside, 0)

    for n, dy in enumerate(reversed(odd)):
        wait_plane(s3, r3, zs, send3, recv3.at[y_at(dy)]).wait_recv()
        block = r3[pl.ds(y_at(dy) * zs, zs)].reshape(zs * qs * 2, sd)
        s4[:, pl.ds(y_at(dy), 1)] = dot(moves[3], block).astype(BF16).reshape(qs, 1, 2 * zs, sd)
        to_chip(s4, r4, y_at(dy), send4, recv4.at[n])

    wait_ctx(u_own, u_all, send_u, recv_u).wait_recv()
    decay = jnp.exp(-rate_rows[me] * float(sd))
    state = jnp.zeros((1, cb), F32)
    for p in range(nc - 1, -1, -1):
        st_own[p] = state
        state = u_all[p] + decay * state
    send_to_ctx(st_own, st_all, send_s, recv_s)

    for n in (6, 7, 8, 9):
        loads[n].wait()
    turn_c, turn_s = twist[0], twist[1]

    def transform(part_of_y):
        half = xs * nc
        for share in range(xs):
            for arr in range(2):
                part = [blocks[a * yls + part_of_y, share * 2 + arr] for a in range(yhs)]
                freq = dot(first[...], jnp.concatenate(part + part, axis=0))
                re, im = freq[:nc], freq[nc:]
                high_re, low_re = split(re * turn_c + im * turn_s)
                high_im, low_im = split(im * turn_c - re * turn_s)
                to = pl.ds(arr * half + share * nc, nc)
                for n, piece in enumerate((high_re, high_im, low_re, low_im)):
                    left[to, n * sd : (n + 1) * sd] = piece
        both = dot(left[...], second[: 4 * sd]) + dot(left[:, : 2 * sd], second[4 * sd :])
        x_re, x_im = both[:half, :sd], both[:half, sd:]
        g_re, g_im = both[half:, :sd], both[half:, sd:]
        re = x_re * g_re + x_im * g_im
        im = x_re * g_im - x_im * g_re
        total_re = sum(re[n * nc : (n + 1) * nc] for n in range(xs))
        total_im = sum(im[n * nc : (n + 1) * nc] for n in range(xs))
        return total_re, total_im

    for n, dy in enumerate(reversed(odd)):
        wait_chip(s4, r4, send4, recv4.at[n]).wait_recv()
        block = r4[:, pl.ds(y_at(dy), 1)].reshape(qs * 2 * zs, sd)
        blocks[pl.ds(y_at(dy), 1)] = dot(moves[4], block).astype(BF16).reshape(1, xs * 2, run, sd)
    for d in range(1, yls):
        spec[:, :sd], spec[:, sd:] = transform(lax.rem(yl + d, yls))
    for dy in reversed(even):
        wait_plane(s2, r2, zs if dy else zs - 1, send2, recv2.at[y_at(dy)]).wait_recv()
        block = r2[pl.ds(y_at(dy) * zs, zs)].reshape(zs * qs * 2, sd)
        blocks[pl.ds(y_at(dy), 1)] = dot(moves[1], block).astype(BF16).reshape(1, xs * 2, run, sd)
    spec_re, spec_im = transform(yl)
    spec_re, spec_im = spec_re + spec[:, :sd], spec_im + spec[:, sd:]

    re_h, re_l = split(spec_re)
    im_h, im_l = split(-spec_im)
    both = dot(jnp.concatenate([re_h, im_h, re_l, im_l, re_h, im_h], axis=1), second[...])
    re, im = both[:, :sd], -both[:, sd:]
    high, low = split(
        jnp.concatenate([re * turn_c - im * turn_s, im * turn_c + re * turn_s], axis=0)
    )
    scale = 2.0 / (2 * nc * sd) / math.sqrt(nc * sd * nh)
    result = dot(last[...], jnp.concatenate([high, low, high], axis=0)) * scale
    for d in range(nc):
        t_own[d] = result[d : d + 1]
    send_to_ctx(t_own, t_all, send_t, recv_t)

    wait_ctx(st_own, st_all, send_s, recv_s).wait_recv()

    def outside(blk, _):
        at = columns(blk)
        rate = rate_ref[:, at]
        weight = ww[:, at]
        fine = []
        for n in range(modes):
            carried = weight[n : n + 1] * st_all[n * nblk + blk]
            eb[n] = carried * jnp.exp(-rate[n : n + 1] * (float(sd - 8) - octs))
            fine.append(jnp.exp(-rate[n : n + 1] * (8.0 - eight)))
        for t in range(tiles):
            total = y[8 * t : 8 * t + 8, at]
            for n in range(modes):
                total = total + jnp.broadcast_to(eb[n, t : t + 1], (8, cb)) * fine[n]
            y[8 * t : 8 * t + 8, at] = total
        return 0

    lax.fori_loop(0, nblk, outside, 0)

    leave = pltpu.make_async_copy(y, y_ref, y_sem)
    leave.start()

    wait_ctx(t_own, t_all, send_t, recv_t).wait_recv()
    gathered = jnp.concatenate([t_all[d] for d in range(nc)], axis=0)
    out_ref[...] = gathered

    leave.wait()
    for source, target, send in ((s1, r1, send1), (s4, r4, send4)):
        some = (pl.ds(0, qs - 1), pl.ds(0, len(even)))
        copy(some_chip, source.at[some], target.at[some], send, recv1.at[0]).wait_send()
    wait_plane(s2, r2, len(even) * zs - 1, send2, recv2.at[0]).wait_send()
    wait_plane(s3, r3, len(odd) * zs, send3, recv3.at[0]).wait_send()
    wait_ctx(u_own, u_all, send_u, recv_u).wait_send()
    wait_ctx(st_own, st_all, send_s, recv_s).wait_send()
    wait_ctx(t_own, t_all, send_t, recv_t).wait_send()


def finish(input_in, filter_in, input_out, filter_out):
    input_out[...] = input_in[...]
    filter_out[...] = filter_in[...]


def body(nc, nh, inputs, out_grad, decay_rate, residue, skip_gain):
    sd, cols = inputs.shape
    modes = decay_rate.shape[0]
    cb = modes * cols // nc
    args = (inputs, out_grad, decay_rate, residue, skip_gain.reshape(1, cols))
    args += tuple(jnp.asarray(t) for t in tables(nc, nh, sd))
    yhs, zs, cores, yls, xs = shape_of(nc, nh)
    ys, qs = yhs * yls, cores * xs
    vmem = pl.BlockSpec(memory_space=pltpu.VMEM)
    dma = pltpu.SemaphoreType.DMA
    input_grad, filter_grad = pl.pallas_call(
        functools.partial(kernel, nc, nh, modes),
        out_shape=(
            jax.ShapeDtypeStruct((sd, cols), F32),
            jax.ShapeDtypeStruct((nc, sd), F32),
        ),
        in_specs=[pl.BlockSpec(memory_space=pltpu.HBM)] * len(args),
        out_specs=(pl.BlockSpec(memory_space=pltpu.HBM), vmem),
        scratch_shapes=[pltpu.VMEM(arg.shape, arg.dtype) for arg in args]
        + [
            pltpu.VMEM((2, cols // (zs * cores), zs * cores, sd), BF16),
            pltpu.VMEM((qs, ys, 2 * zs, sd), BF16),
            pltpu.VMEM((qs, ys, 2 * zs, sd), BF16),
            pltpu.VMEM((ys * zs, qs * 2, sd), BF16),
            pltpu.VMEM((ys * zs, qs * 2, sd), BF16),
            pltpu.VMEM((ys * zs, qs * 2, sd), BF16),
            pltpu.VMEM((ys * zs, qs * 2, sd), BF16),
            pltpu.VMEM((qs, ys, 2 * zs, sd), BF16),
            pltpu.VMEM((qs, ys, 2 * zs, sd), BF16),
            pltpu.VMEM((nc, 1, cb), F32),
            pltpu.VMEM((nc, 1, cb), F32),
            pltpu.VMEM((nc, 1, cb), F32),
            pltpu.VMEM((nc, 1, cb), F32),
            pltpu.VMEM((nc, 1, sd), F32),
            pltpu.VMEM((nc, 1, sd), F32),
            pltpu.VMEM((sd, cols), F32),
            pltpu.VMEM((sd, cols), F32),
            pltpu.VMEM((sd, cols), F32),
            pltpu.VMEM((modes, sd // 8, cb), F32),
            pltpu.VMEM((modes, cols), F32),
            pltpu.VMEM((nc, 1, cb), F32),
            pltpu.VMEM((ys, xs * 2, zs * cores, sd), BF16),
            pltpu.VMEM((2 * xs * nc, 4 * sd), BF16),
            pltpu.VMEM((nc, 2 * sd), F32),
            dma((len(args),)),
            dma((ys,)),
            dma((ys,)),
            dma((ys,)),
            dma((ys,)),
        ]
        + [dma] * 11,
        compiler_params=pltpu.CompilerParams(
            collective_id=0, has_side_effects=True, vmem_limit_bytes=64 * 1024 * 1024
        ),
        name="modal_backward",
    )(*args)
    input_grad, filter_grad = pl.pallas_call(
        finish,
        out_shape=(jax.ShapeDtypeStruct((sd, cols), F32), jax.ShapeDtypeStruct((nc, sd), F32)),
        in_specs=[vmem, vmem],
        out_specs=(vmem, vmem),
        compiler_params=pltpu.CompilerParams(vmem_limit_bytes=64 * 1024 * 1024),
        name="finish",
    )(input_grad, filter_grad)
    return input_grad, filter_grad.T


def solution(mesh):
    placed = (P("ctx", "ch"), P("ctx", "ch"), P(), P(), P("ch"))
    return jax.shard_map(
        functools.partial(body, mesh.shape["ctx"], mesh.shape["ch"]),
        mesh=mesh,
        in_specs=placed,
        out_specs=(P("ctx", "ch"), P("ctx", "ch")),
        check_vma=False,
    )
```

```python
import functools
import math

import jax
import jax.numpy as jnp
import ml_dtypes
import numpy as np
from jax import lax
from jax.experimental import pallas as pl
from jax.experimental.pallas import tpu as pltpu
from jax.sharding import PartitionSpec as P

MESH = pl.DeviceIdType.MESH
F32 = jnp.float32
BF16 = jnp.bfloat16


def shape_of(nc, nh):
    z = nc // 8 if nc >= 32 else nc // 4
    x = nh // 2
    return nc // (2 * z), z, 2, nh // x, x


def halves(table):
    high = table.astype(np.float32).astype(ml_dtypes.bfloat16)
    low = (table - high.astype(np.float64)).astype(np.float32).astype(ml_dtypes.bfloat16)
    return high, low


def reorder(sizes, old, new):
    count = np.arange(math.prod(sizes[axis] for axis in old)).reshape([sizes[axis] for axis in old])
    moved = count.transpose([old.index(axis) for axis in new]).reshape(-1)
    return np.eye(moved.size, dtype=np.float32)[moved]


@functools.lru_cache(maxsize=None)
def tables(nc, nh, sd):
    _, zs, cores, _, xs = shape_of(nc, nh)
    j = np.arange(nc) + 0.5
    a = np.arange(nc)
    s = np.arange(sd)
    full = 2 * nc * sd
    angle = 2.0 * np.pi * np.outer(j, a) / (2 * nc)
    block = np.concatenate([np.cos(angle), -np.sin(angle)], axis=0)
    high, low = halves(block)
    first = np.concatenate([high, low], axis=1)
    last_h, last_l = halves(block.T.copy())
    last = np.concatenate([last_h, last_h, last_l], axis=1)
    angle = 2.0 * np.pi * np.outer(j, s) / full
    twist = np.stack([np.cos(angle), np.sin(angle)]).astype(np.float32)
    angle = 2.0 * np.pi * (np.outer(s, s) % sd) / sd
    cos, sin = np.cos(angle), np.sin(angle)
    step = np.concatenate([np.concatenate([cos, -sin], axis=1), np.concatenate([sin, cos], axis=1)], axis=0)
    high, low = halves(step)
    second = np.concatenate([high, high, low], axis=0)
    angle = 2.0 * np.pi * np.outer(s + 0.5, s) / (2 * sd)
    near = np.concatenate([np.cos(angle), -np.sin(angle)], axis=0)
    high, low = halves(near)
    near_in = np.concatenate([high, low, high], axis=1)
    near_out = np.concatenate([high.T, high.T, low.T], axis=1)
    qx = {"q": cores * xs, "core": cores, "x": xs, "arr": 2, "z": zs}
    moves = [
        reorder(qx, ("core", "x", "arr", "z"), ("z", "core", "x", "arr")),
        reorder(qx, ("z", "core", "x", "arr"), ("x", "arr", "z", "core")),
        reorder(qx, ("arr", "x", "core", "z"), ("z", "arr", "core", "x")),
        reorder(qx, ("z", "arr", "core", "x"), ("core", "x", "arr", "z")),
        reorder(qx, ("core", "x", "arr", "z"), ("x", "arr", "z", "core")),
    ]
    bf = ml_dtypes.bfloat16
    return (
        np.stack(moves).astype(bf),
        first,
        np.ascontiguousarray(second),
        last,
        twist,
        near_in,
        np.ascontiguousarray(near_out),
    )


def split(value):
    high = value.astype(BF16)
    return high, (value - high.astype(F32)).astype(BF16)


def dot(left, right):
    return jnp.dot(left, right, preferred_element_type=F32)


def kernel(nc, nh, modes, *refs):
    args_in, refs = refs[:12], refs[12:]
    (y_ref, out_ref), refs = refs[:2], refs[2:]
    args, refs = refs[:12], refs[12:]
    x_ref, g_ref, rate_ref, res_ref, gain_ref, moves, first, second, last, twist, near_in, near_out = args
    (runs, s1, r1, s2, r2, s3, r3, s4, r4), refs = refs[:9], refs[9:]
    (u_own, u_all, st_own, st_all, t_own, t_all), refs = refs[:6], refs[6:]
    (y, grad, taps, eb, ww, rate_rows, blocks, left, spec), refs = refs[:9], refs[9:]
    (table_sem, recv1, recv2, recv3, recv4, y_sem, send1, send2, send3, send4, send_u, recv_u, send_s, recv_s, send_t, recv_t) = refs

    sd, cols = x_ref.shape
    cb = modes * cols // nc
    nblk = cols // cb
    tiles = sd // 8
    yhs, zs, cores, yls, xs = shape_of(nc, nh)
    ys, qs, run = yhs * yls, cores * xs, zs * cores
    me = lax.axis_index("ctx")
    my = lax.axis_index("ch")
    yh, z, core = me // run, lax.rem(me, run) // cores, lax.rem(me, cores)
    yl, x = my // xs, lax.rem(my, xs)
    y_me = yh * yls + yl
    q_me = core * xs + x

    def farthest(count):
        return sorted(range(count), key=lambda d: -min(d, count - d))

    far_y = farthest(ys)
    even = [dy for dy in far_y if dy % yls == 0]
    odd = [dy for dy in far_y if dy % yls]
    q_steps = [(dc, dx) for dx in farthest(xs) for dc in (1, 0)][:-1]

    def z_at(m):
        return lax.rem(z + zs // 2 + ((m + 1) // 2) * (2 * lax.rem(m, 2) - 1) + zs, zs)

    def y_at(dy):
        return lax.rem(y_me + dy, ys)

    def plane_peer(dy, m):
        there = y_at(dy)
        device = {"ctx": (there // yls * zs + z_at(m)) * cores + core, "ch": lax.rem(there, yls) * xs + x}
        return device, there * zs + z_at(m)

    def chip_peer(step):
        dc, dx = step
        core_at, x_at = lax.rem(core + dc, cores), lax.rem(x + dx, xs)
        return {"ctx": me - core + core_at, "ch": yl * xs + x_at}, core_at * xs + x_at

    def ctx_peer(dyh, t):
        return (lax.rem(yh + dyh, yhs) * zs + z_at(t // cores)) * cores + lax.rem(core + 1 - lax.rem(t, cores), cores)

    def each_plane(dy, act):
        def body(m, _):
            act(*plane_peer(dy, m))
            return 0

        lax.fori_loop(0, zs if dy else zs - 1, body, 0)

    def each_ctx(dyh, act):
        def body(t, _):
            act(ctx_peer(dyh, t))
            return 0

        lax.fori_loop(0, run if dyh else run - 1, body, 0)

    barrier = pltpu.get_barrier_semaphore()

    def greet(device, _):
        pl.semaphore_signal(barrier, inc=1, device_id=device, device_id_type=MESH)

    loads = [
        pltpu.make_async_copy(src, dst, table_sem.at[n]) for n, (src, dst) in enumerate(zip(args_in, args))
    ]
    def greet_other_core(dyh):
        def other(m, _):
            device = (lax.rem(yh + dyh, yhs) * zs + z_at(m)) * cores + lax.rem(core + 1, cores)
            greet({"ctx": device}, 0)
            return 0

        lax.fori_loop(0, zs if dyh else zs - 1, other, 0)

    for n, dy in enumerate(far_y):
        each_plane(dy, greet)
        if dy % yls == 0:
            greet_other_core(dy // yls)
        if n == 0:
            for load in loads[:5]:
                load.start()
    for step in q_steps:
        greet(*chip_peer(step))

    for load in loads[5:]:
        load.start()

    width = min(cols, 256)
    row = lax.broadcasted_iota(jnp.int32, (width, width), 0)
    turn = (
        (row & -run) + (row & (zs - 1)) * cores + ((row & (run - 1)) // zs)
        == lax.broadcasted_iota(jnp.int32, (width, width), 1)
    ).astype(F32).astype(BF16)
    loads[0].wait()
    loads[1].wait()
    for c0 in range(0, cols, width):
        pair_of = [
            lax.dot_general(turn, ref[:, c0 : c0 + width], (((1,), (1,)), ((), ())), preferred_element_type=F32)
            for ref in (x_ref, g_ref)
        ]
        for r0 in range(0, width, zs):
            c = c0 + r0
            to_core = c % run // zs
            to_yh = c // run % yhs
            to_yl, to_x = c // nc // xs, c // nc % xs
            both = jnp.concatenate([part[r0 : r0 + zs] for part in pair_of], axis=0)
            s1[to_core * xs + to_x, to_yh * yls + to_yl] = both.astype(BF16)
        for r0 in range(0, width, run):
            for arr in range(2):
                runs[arr, (c0 + r0) // run] = pair_of[arr][r0 : r0 + run].astype(BF16)

    def copy(device, src, dst, send, recv):
        return pltpu.make_async_remote_copy(
            src_ref=src, dst_ref=dst, send_sem=send, recv_sem=recv, device_id=device, device_id_type=MESH
        )

    some_chip, _ = chip_peer(q_steps[0])
    some_plane, _ = plane_peer(far_y[0], 0)

    def ctx_copy(peer, src, dst, send, recv):
        return copy({"ctx": peer}, src, dst, send, recv)

    def send_to_ctx(own, everyone, send, recv):
        for dyh in farthest(yhs):
            each_ctx(dyh, lambda peer: ctx_copy(peer, own.at[peer], everyone.at[me], send, recv).start())
        everyone[pl.ds(me, 1)] = own[pl.ds(me, 1)]

    def wait_ctx(own, everyone, send, recv, count=nc - 1):
        return ctx_copy(ctx_peer(0, 0), own.at[pl.ds(0, count)], everyone.at[pl.ds(0, count)], send, recv)

    pl.semaphore_wait(barrier, (ys * zs - 1) + (qs - 1) + (yhs * zs - 1))

    def to_chip(source, target, y, send, recv):
        for step in q_steps:
            device, q_at = chip_peer(step)
            copy(device, source.at[q_at, y], target.at[q_me, y], send, recv).start()
        target[pl.ds(q_me, 1), pl.ds(y, 1)] = source[pl.ds(q_me, 1), pl.ds(y, 1)]

    def to_plane(source, target, dy, send, recv):
        def onward(device, at):
            copy(device, source.at[at], target.at[y_me * zs + z], send, recv).start()

        each_plane(dy, onward)

    def wait_chip(source, target, send, recv):
        return copy(some_chip, source.at[pl.ds(0, qs - 1), 0], target.at[pl.ds(0, qs - 1), 0], send, recv)

    def wait_plane(source, target, count, send, recv):
        return copy(some_plane, source.at[pl.ds(0, count)], target.at[pl.ds(0, count)], send, recv)

    for n, dy in enumerate(even):
        to_chip(s1, r1, y_at(dy), send1, recv1.at[n])
    loads[5].wait()
    for dy in odd:
        there = y_at(dy)
        first_run = lax.rem(there, yls) * xs * yhs + there // yls
        piece = [runs[arr, first_run + to_x * yhs] for arr in range(2) for to_x in range(xs)]
        piece = dot(moves[2], jnp.concatenate(piece, axis=0))
        s3[pl.ds(there * zs, zs)] = piece.astype(BF16).reshape(zs, qs * 2, sd)

    def both_ways(m, _):
        for dy in odd:
            device, at = plane_peer(dy, m)
            copy(device, s3.at[at], r3.at[y_me * zs + z], send3, recv3.at[y_me]).start()
        return 0

    lax.fori_loop(0, zs, both_ways, 0)

    for n in (2, 3, 4):
        loads[n].wait()

    grad[...] = g_ref[...].astype(F32)
    eight = lax.broadcasted_iota(jnp.int32, (8, cb), 0).astype(F32)
    octs = 8.0 * lax.broadcasted_iota(jnp.int32, (tiles, cb), 0).astype(F32)

    def weight_of(rate, residue):
        x = 2.0 * rate
        series = 1.0 - x * (1.0 / 7.0)
        for n in (6, 5, 4, 3, 2):
            series = 1.0 - (x * (1.0 / n)) * series
        return residue * jnp.sqrt(x * series)

    def columns(blk):
        return pl.ds(pl.multiple_of(blk * cb, cb), cb)

    def states(blk, _):
        at = columns(blk)
        rate = rate_ref[:, at]
        weight = weight_of(rate, res_ref[:, at])
        ww[:, at] = weight
        for n in range(modes):
            slow = jnp.exp(-rate[n : n + 1] * octs)
            eb[n] = slow
        fine = [jnp.exp(-rate[n : n + 1] * eight) for n in range(modes)]
        scaled = [fine[n] * weight[n : n + 1] for n in range(modes)]
        sums = [jnp.zeros((8, cb), F32) for _ in range(modes)]
        for t in range(tiles):
            g = grad[8 * t : 8 * t + 8, at]
            tap = jnp.zeros((8, cb), F32)
            for n in range(modes):
                level = jnp.broadcast_to(eb[n, t : t + 1], (8, cb))
                sums[n] = sums[n] + level * g
                tap = tap + level * scaled[n]
            taps[8 * t : 8 * t + 8, at] = tap
        for n in range(modes):
            rate_rows[n * nblk + blk] = rate[n : n + 1]
            u_own[n * nblk + blk] = jnp.sum(sums[n] * fine[n], axis=0, keepdims=True)
        return 0

    lax.fori_loop(0, nblk, states, 0)

    send_to_ctx(u_own, u_all, send_u, recv_u)

    for n, dy in enumerate(even):
        wait_chip(s1, r1, send1, recv1.at[n]).wait_recv()
        block = r1[:, pl.ds(y_at(dy), 1)].reshape(qs * 2 * zs, sd)
        s2[pl.ds(y_at(dy) * zs, zs)] = dot(moves[0], block).astype(BF16).reshape(zs, qs * 2, sd)
        to_plane(s2, r2, dy, send2, recv2.at[y_me])
    own = pl.ds(y_me * zs + z, 1)
    r2[own] = s2[own]

    loads[10].wait()
    loads[11].wait()
    wide = min(cols, 256)

    def inside(blk, _):
        at = pl.ds(pl.multiple_of(blk * wide, wide), wide)
        g = g_ref[:, at]
        g_spec = dot(near_in[:, : 2 * sd], jnp.concatenate([g, g], axis=0))
        high, low = split(taps[:, at])
        h_spec = dot(near_in[...], jnp.concatenate([high, high, low], axis=0))
        g_re, g_im = g_spec[:sd], g_spec[sd:]
        h_re, h_im = h_spec[:sd], h_spec[sd:]
        term = jnp.concatenate([h_re * g_re + h_im * g_im, h_re * g_im - h_im * g_re], axis=0)
        high, low = split(term)
        part = dot(near_out[...], jnp.concatenate([high, low, high], axis=0)) * (1.0 / sd)
        y[:, at] = part + gain_ref[:, at] * grad[:, at]
        return 0

    lax.fori_loop(0, cols // wide, inside, 0)

    for n, dy in enumerate(reversed(odd)):
        wait_plane(s3, r3, zs, send3, recv3.at[y_at(dy)]).wait_recv()
        block = r3[pl.ds(y_at(dy) * zs, zs)].reshape(zs * qs * 2, sd)
        s4[:, pl.ds(y_at(dy), 1)] = dot(moves[3], block).astype(BF16).reshape(qs, 1, 2 * zs, sd)
        to_chip(s4, r4, y_at(dy), send4, recv4.at[n])

    wait_ctx(u_own, u_all, send_u, recv_u).wait_recv()
    decay = jnp.exp(-rate_rows[me] * float(sd))
    state = jnp.zeros((1, cb), F32)
    for p in range(nc - 1, -1, -1):
        st_own[p] = state
        state = u_all[p] + decay * state
    send_to_ctx(st_own, st_all, send_s, recv_s)

    for n in (6, 7, 8, 9):
        loads[n].wait()
    turn_c, turn_s = twist[0], twist[1]

    def transform(part_of_y):
        half = xs * nc
        for share in range(xs):
            for arr in range(2):
                part = [blocks[a * yls + part_of_y, share * 2 + arr] for a in range(yhs)]
                freq = dot(first[...], jnp.concatenate(part + part, axis=0))
                re, im = freq[:nc], freq[nc:]
                high_re, low_re = split(re * turn_c + im * turn_s)
                high_im, low_im = split(im * turn_c - re * turn_s)
                to = pl.ds(arr * half + share * nc, nc)
                for n, piece in enumerate((high_re, high_im, low_re, low_im)):
                    left[to, n * sd : (n + 1) * sd] = piece
        both = dot(left[...], second[: 4 * sd]) + dot(left[:, : 2 * sd], second[4 * sd :])
        x_re, x_im = both[:half, :sd], both[:half, sd:]
        g_re, g_im = both[half:, :sd], both[half:, sd:]
        re = x_re * g_re + x_im * g_im
        im = x_re * g_im - x_im * g_re
        total_re = sum(re[n * nc : (n + 1) * nc] for n in range(xs))
        total_im = sum(im[n * nc : (n + 1) * nc] for n in range(xs))
        return total_re, total_im

    for n, dy in enumerate(reversed(odd)):
        wait_chip(s4, r4, send4, recv4.at[n]).wait_recv()
        block = r4[:, pl.ds(y_at(dy), 1)].reshape(qs * 2 * zs, sd)
        blocks[pl.ds(y_at(dy), 1)] = dot(moves[4], block).astype(BF16).reshape(1, xs * 2, run, sd)
    for d in range(1, yls):
        spec[:, :sd], spec[:, sd:] = transform(lax.rem(yl + d, yls))
    for dy in reversed(even):
        wait_plane(s2, r2, zs if dy else zs - 1, send2, recv2.at[y_at(dy)]).wait_recv()
        block = r2[pl.ds(y_at(dy) * zs, zs)].reshape(zs * qs * 2, sd)
        blocks[pl.ds(y_at(dy), 1)] = dot(moves[1], block).astype(BF16).reshape(1, xs * 2, run, sd)
    spec_re, spec_im = transform(yl)
    spec_re, spec_im = spec_re + spec[:, :sd], spec_im + spec[:, sd:]

    re_h, re_l = split(spec_re)
    im_h, im_l = split(-spec_im)
    both = dot(jnp.concatenate([re_h, im_h, re_l, im_l, re_h, im_h], axis=1), second[...])
    re, im = both[:, :sd], -both[:, sd:]
    high, low = split(
        jnp.concatenate([re * turn_c - im * turn_s, im * turn_c + re * turn_s], axis=0)
    )
    scale = 2.0 / (2 * nc * sd) / math.sqrt(nc * sd * nh)
    result = dot(last[...], jnp.concatenate([high, low, high], axis=0)) * scale
    for d in range(nc):
        t_own[d] = result[d : d + 1]
    send_to_ctx(t_own, t_all, send_t, recv_t)

    wait_ctx(st_own, st_all, send_s, recv_s).wait_recv()

    def outside(blk, _):
        at = columns(blk)
        rate = rate_ref[:, at]
        weight = ww[:, at]
        fine = []
        for n in range(modes):
            carried = weight[n : n + 1] * st_all[n * nblk + blk]
            eb[n] = carried * jnp.exp(-rate[n : n + 1] * (float(sd - 8) - octs))
            fine.append(jnp.exp(-rate[n : n + 1] * (8.0 - eight)))
        for t in range(tiles):
            total = y[8 * t : 8 * t + 8, at]
            for n in range(modes):
                total = total + jnp.broadcast_to(eb[n, t : t + 1], (8, cb)) * fine[n]
            y[8 * t : 8 * t + 8, at] = total
        return 0

    lax.fori_loop(0, nblk, outside, 0)

    leave = pltpu.make_async_copy(y, y_ref, y_sem)
    leave.start()

    wait_ctx(t_own, t_all, send_t, recv_t).wait_recv()
    gathered = jnp.concatenate([t_all[d] for d in range(nc)], axis=0)
    out_ref[...] = gathered

    leave.wait()
    for source, target, send in ((s1, r1, send1), (s4, r4, send4)):
        some = (pl.ds(0, qs - 1), pl.ds(0, len(even)))
        copy(some_chip, source.at[some], target.at[some], send, recv1.at[0]).wait_send()
    wait_plane(s2, r2, len(even) * zs - 1, send2, recv2.at[0]).wait_send()
    wait_plane(s3, r3, len(odd) * zs, send3, recv3.at[0]).wait_send()
    wait_ctx(u_own, u_all, send_u, recv_u).wait_send()
    wait_ctx(st_own, st_all, send_s, recv_s).wait_send()
    wait_ctx(t_own, t_all, send_t, recv_t).wait_send()


def finish(input_in, filter_in, input_out, filter_out):
    input_out[...] = input_in[...]
    filter_out[...] = filter_in[...]


def body(nc, nh, inputs, out_grad, decay_rate, residue, skip_gain):
    sd, cols = inputs.shape
    modes = decay_rate.shape[0]
    cb = modes * cols // nc
    args = (inputs, out_grad, decay_rate, residue, skip_gain.reshape(1, cols))
    args += tuple(jnp.asarray(t) for t in tables(nc, nh, sd))
    yhs, zs, cores, yls, xs = shape_of(nc, nh)
    ys, qs = yhs * yls, cores * xs
    vmem = pl.BlockSpec(memory_space=pltpu.VMEM)
    dma = pltpu.SemaphoreType.DMA
    input_grad, filter_grad = pl.pallas_call(
        functools.partial(kernel, nc, nh, modes),
        out_shape=(
            jax.ShapeDtypeStruct((sd, cols), F32),
            jax.ShapeDtypeStruct((nc, sd), F32),
        ),
        in_specs=[pl.BlockSpec(memory_space=pltpu.HBM)] * len(args),
        out_specs=(pl.BlockSpec(memory_space=pltpu.HBM), vmem),
        scratch_shapes=[pltpu.VMEM(arg.shape, arg.dtype) for arg in args]
        + [
            pltpu.VMEM((2, cols // (zs * cores), zs * cores, sd), BF16),
            pltpu.VMEM((qs, ys, 2 * zs, sd), BF16),
            pltpu.VMEM((qs, ys, 2 * zs, sd), BF16),
            pltpu.VMEM((ys * zs, qs * 2, sd), BF16),
            pltpu.VMEM((ys * zs, qs * 2, sd), BF16),
            pltpu.VMEM((ys * zs, qs * 2, sd), BF16),
            pltpu.VMEM((ys * zs, qs * 2, sd), BF16),
            pltpu.VMEM((qs, ys, 2 * zs, sd), BF16),
            pltpu.VMEM((qs, ys, 2 * zs, sd), BF16),
            pltpu.VMEM((nc, 1, cb), F32),
            pltpu.VMEM((nc, 1, cb), F32),
            pltpu.VMEM((nc, 1, cb), F32),
            pltpu.VMEM((nc, 1, cb), F32),
            pltpu.VMEM((nc, 1, sd), F32),
            pltpu.VMEM((nc, 1, sd), F32),
            pltpu.VMEM((sd, cols), F32),
            pltpu.VMEM((sd, cols), F32),
            pltpu.VMEM((sd, cols), F32),
            pltpu.VMEM((modes, sd // 8, cb), F32),
            pltpu.VMEM((modes, cols), F32),
            pltpu.VMEM((nc, 1, cb), F32),
            pltpu.VMEM((ys, xs * 2, zs * cores, sd), BF16),
            pltpu.VMEM((2 * xs * nc, 4 * sd), BF16),
            pltpu.VMEM((nc, 2 * sd), F32),
            dma((len(args),)),
            dma((ys,)),
            dma((ys,)),
            dma((ys,)),
            dma((ys,)),
        ]
        + [dma] * 11,
        compiler_params=pltpu.CompilerParams(
            collective_id=0, has_side_effects=True, vmem_limit_bytes=64 * 1024 * 1024
        ),
        name="modal_backward",
    )(*args)
    input_grad, filter_grad = pl.pallas_call(
        finish,
        out_shape=(jax.ShapeDtypeStruct((sd, cols), F32), jax.ShapeDtypeStruct((nc, sd), F32)),
        in_specs=[vmem, vmem],
        out_specs=(vmem, vmem),
        compiler_params=pltpu.CompilerParams(vmem_limit_bytes=64 * 1024 * 1024),
        name="finish",
    )(input_grad, filter_grad)
    return input_grad, filter_grad.T


def solution(mesh):
    placed = (P("ctx", "ch"), P("ctx", "ch"), P(), P(), P("ch"))
    return jax.shard_map(
        functools.partial(body, mesh.shape["ctx"], mesh.shape["ch"]),
        mesh=mesh,
        in_specs=placed,
        out_specs=(P("ctx", "ch"), P("ctx", "ch")),
        check_vma=False,
    )
```

```python
import functools
import math

import jax
import jax.numpy as jnp
import ml_dtypes
import numpy as np
from jax import lax
from jax.experimental import pallas as pl
from jax.experimental.pallas import tpu as pltpu
from jax.sharding import PartitionSpec as P

MESH = pl.DeviceIdType.MESH
F32 = jnp.float32
BF16 = jnp.bfloat16


def shape_of(nc, nh):
    z = nc // 8 if nc >= 32 else nc // 4
    x = nh // 2
    return nc // (2 * z), z, 2, nh // x, x


def halves(table):
    high = table.astype(np.float32).astype(ml_dtypes.bfloat16)
    low = (table - high.astype(np.float64)).astype(np.float32).astype(ml_dtypes.bfloat16)
    return high, low


def reorder(sizes, old, new):
    count = np.arange(math.prod(sizes[axis] for axis in old)).reshape([sizes[axis] for axis in old])
    moved = count.transpose([old.index(axis) for axis in new]).reshape(-1)
    return np.eye(moved.size, dtype=np.float32)[moved]


@functools.lru_cache(maxsize=None)
def tables(nc, nh, sd):
    _, zs, cores, _, xs = shape_of(nc, nh)
    j = np.arange(nc) + 0.5
    a = np.arange(nc)
    s = np.arange(sd)
    full = 2 * nc * sd
    angle = 2.0 * np.pi * np.outer(j, a) / (2 * nc)
    block = np.concatenate([np.cos(angle), -np.sin(angle)], axis=0)
    high, low = halves(block)
    first = np.concatenate([high, low], axis=1)
    last_h, last_l = halves(block.T.copy())
    last = np.concatenate([last_h, last_h, last_l], axis=1)
    angle = 2.0 * np.pi * np.outer(j, s) / full
    twist = np.stack([np.cos(angle), np.sin(angle)]).astype(np.float32)
    angle = 2.0 * np.pi * (np.outer(s, s) % sd) / sd
    cos, sin = np.cos(angle), np.sin(angle)
    step = np.concatenate([np.concatenate([cos, -sin], axis=1), np.concatenate([sin, cos], axis=1)], axis=0)
    high, low = halves(step)
    second = np.concatenate([high, high, low], axis=0)
    angle = 2.0 * np.pi * np.outer(s + 0.5, s) / (2 * sd)
    near = np.concatenate([np.cos(angle), -np.sin(angle)], axis=0)
    high, low = halves(near)
    near_in = np.concatenate([high, low, high], axis=1)
    near_out = np.concatenate([high.T, high.T, low.T], axis=1)
    qx = {"q": cores * xs, "core": cores, "x": xs, "arr": 2, "z": zs}
    moves = [
        reorder(qx, ("core", "x", "arr", "z"), ("z", "core", "x", "arr")),
        reorder(qx, ("z", "core", "x", "arr"), ("x", "arr", "z", "core")),
        reorder(qx, ("arr", "x", "core", "z"), ("z", "arr", "core", "x")),
        reorder(qx, ("z", "arr", "core", "x"), ("core", "x", "arr", "z")),
        reorder(qx, ("core", "x", "arr", "z"), ("x", "arr", "z", "core")),
    ]
    bf = ml_dtypes.bfloat16
    return (
        np.stack(moves).astype(bf),
        first,
        np.ascontiguousarray(second),
        last,
        twist,
        near_in,
        np.ascontiguousarray(near_out),
    )


def split(value):
    high = value.astype(BF16)
    return high, (value - high.astype(F32)).astype(BF16)


def dot(left, right):
    return jnp.dot(left, right, preferred_element_type=F32)


def kernel(nc, nh, modes, *refs):
    args_in, refs = refs[:12], refs[12:]
    (y_ref, out_ref), refs = refs[:2], refs[2:]
    args, refs = refs[:12], refs[12:]
    x_ref, g_ref, rate_ref, res_ref, gain_ref, moves, first, second, last, twist, near_in, near_out = args
    (runs, s1, r1, s2, r2, s3, r3, s4, r4), refs = refs[:9], refs[9:]
    (u_own, u_all, st_own, st_all, t_own, t_all), refs = refs[:6], refs[6:]
    (y, grad, taps, eb, ww, rate_rows, blocks, left, spec), refs = refs[:9], refs[9:]
    (table_sem, recv1, recv2, recv3, recv4, y_sem, send1, send2, send3, send4, send_u, recv_u, send_s, recv_s, send_t, recv_t) = refs

    sd, cols = x_ref.shape
    cb = modes * cols // nc
    nblk = cols // cb
    tiles = sd // 8
    yhs, zs, cores, yls, xs = shape_of(nc, nh)
    ys, qs, run = yhs * yls, cores * xs, zs * cores
    me = lax.axis_index("ctx")
    my = lax.axis_index("ch")
    yh, z, core = me // run, lax.rem(me, run) // cores, lax.rem(me, cores)
    yl, x = my // xs, lax.rem(my, xs)
    y_me = yh * yls + yl
    q_me = core * xs + x

    def farthest(count):
        return sorted(range(count), key=lambda d: -min(d, count - d))

    far_y = farthest(ys)
    even = [dy for dy in far_y if dy % yls == 0]
    odd = [dy for dy in far_y if dy % yls]
    q_steps = [(dc, dx) for dx in farthest(xs) for dc in (1, 0)][:-1]

    def z_at(m):
        return lax.rem(z + zs // 2 + ((m + 1) // 2) * (2 * lax.rem(m, 2) - 1) + zs, zs)

    def y_at(dy):
        return lax.rem(y_me + dy, ys)

    def plane_peer(dy, m):
        there = y_at(dy)
        device = {"ctx": (there // yls * zs + z_at(m)) * cores + core, "ch": lax.rem(there, yls) * xs + x}
        return device, there * zs + z_at(m)

    def chip_peer(step):
        dc, dx = step
        core_at, x_at = lax.rem(core + dc, cores), lax.rem(x + dx, xs)
        return {"ctx": me - core + core_at, "ch": yl * xs + x_at}, core_at * xs + x_at

    def ctx_peer(dyh, t):
        return (lax.rem(yh + dyh, yhs) * zs + z_at(t // cores)) * cores + lax.rem(core + 1 - lax.rem(t, cores), cores)

    def each_plane(dy, act):
        def body(m, _):
            act(*plane_peer(dy, m))
            return 0

        lax.fori_loop(0, zs if dy else zs - 1, body, 0)

    def each_ctx(dyh, act):
        def body(t, _):
            act(ctx_peer(dyh, t))
            return 0

        lax.fori_loop(0, run if dyh else run - 1, body, 0)

    barrier = pltpu.get_barrier_semaphore()

    def greet(device, _):
        pl.semaphore_signal(barrier, inc=1, device_id=device, device_id_type=MESH)

    loads = [
        pltpu.make_async_copy(src, dst, table_sem.at[n]) for n, (src, dst) in enumerate(zip(args_in, args))
    ]
    def greet_other_core(dyh):
        def other(m, _):
            device = (lax.rem(yh + dyh, yhs) * zs + z_at(m)) * cores + lax.rem(core + 1, cores)
            greet({"ctx": device}, 0)
            return 0

        lax.fori_loop(0, zs if dyh else zs - 1, other, 0)

    for n, dy in enumerate(far_y):
        each_plane(dy, greet)
        if dy % yls == 0:
            greet_other_core(dy // yls)
        if n == 0:
            for load in loads[:5]:
                load.start()
    for step in q_steps:
        greet(*chip_peer(step))

    for load in loads[5:]:
        load.start()

    width = min(cols, 256)
    row = lax.broadcasted_iota(jnp.int32, (width, width), 0)
    turn = (
        (row & -run) + (row & (zs - 1)) * cores + ((row & (run - 1)) // zs)
        == lax.broadcasted_iota(jnp.int32, (width, width), 1)
    ).astype(F32).astype(BF16)
    loads[0].wait()
    loads[1].wait()
    for c0 in range(0, cols, width):
        pair_of = [
            lax.dot_general(turn, ref[:, c0 : c0 + width], (((1,), (1,)), ((), ())), preferred_element_type=F32)
            for ref in (x_ref, g_ref)
        ]
        for r0 in range(0, width, zs):
            c = c0 + r0
            to_core = c % run // zs
            to_yh = c // run % yhs
            to_yl, to_x = c // nc // xs, c // nc % xs
            both = jnp.concatenate([part[r0 : r0 + zs] for part in pair_of], axis=0)
            s1[to_core * xs + to_x, to_yh * yls + to_yl] = both.astype(BF16)
        for r0 in range(0, width, run):
            for arr in range(2):
                runs[arr, (c0 + r0) // run] = pair_of[arr][r0 : r0 + run].astype(BF16)

    def copy(device, src, dst, send, recv):
        return pltpu.make_async_remote_copy(
            src_ref=src, dst_ref=dst, send_sem=send, recv_sem=recv, device_id=device, device_id_type=MESH
        )

    some_chip, _ = chip_peer(q_steps[0])
    some_plane, _ = plane_peer(far_y[0], 0)

    def ctx_copy(peer, src, dst, send, recv):
        return copy({"ctx": peer}, src, dst, send, recv)

    def send_to_ctx(own, everyone, send, recv):
        for dyh in farthest(yhs):
            each_ctx(dyh, lambda peer: ctx_copy(peer, own.at[peer], everyone.at[me], send, recv).start())
        everyone[pl.ds(me, 1)] = own[pl.ds(me, 1)]

    def wait_ctx(own, everyone, send, recv, count=nc - 1):
        return ctx_copy(ctx_peer(0, 0), own.at[pl.ds(0, count)], everyone.at[pl.ds(0, count)], send, recv)

    pl.semaphore_wait(barrier, (ys * zs - 1) + (qs - 1) + (yhs * zs - 1))

    def to_chip(source, target, y, send, recv):
        for step in q_steps:
            device, q_at = chip_peer(step)
            copy(device, source.at[q_at, y], target.at[q_me, y], send, recv).start()
        target[pl.ds(q_me, 1), pl.ds(y, 1)] = source[pl.ds(q_me, 1), pl.ds(y, 1)]

    def to_plane(source, target, dy, send, recv):
        def onward(device, at):
            copy(device, source.at[at], target.at[y_me * zs + z], send, recv).start()

        each_plane(dy, onward)

    def wait_chip(source, target, send, recv):
        return copy(some_chip, source.at[pl.ds(0, qs - 1), 0], target.at[pl.ds(0, qs - 1), 0], send, recv)

    def wait_plane(source, target, count, send, recv):
        return copy(some_plane, source.at[pl.ds(0, count)], target.at[pl.ds(0, count)], send, recv)

    for n, dy in enumerate(even):
        to_chip(s1, r1, y_at(dy), send1, recv1.at[n])
    loads[5].wait()
    for dy in odd:
        there = y_at(dy)
        first_run = lax.rem(there, yls) * xs * yhs + there // yls
        piece = [runs[arr, first_run + to_x * yhs] for arr in range(2) for to_x in range(xs)]
        piece = dot(moves[2], jnp.concatenate(piece, axis=0))
        s3[pl.ds(there * zs, zs)] = piece.astype(BF16).reshape(zs, qs * 2, sd)

    def both_ways(m, _):
        for dy in odd:
            device, at = plane_peer(dy, m)
            copy(device, s3.at[at], r3.at[y_me * zs + z], send3, recv3.at[y_me]).start()
        return 0

    lax.fori_loop(0, zs, both_ways, 0)

    for n in (2, 3, 4):
        loads[n].wait()

    grad[...] = g_ref[...].astype(F32)
    eight = lax.broadcasted_iota(jnp.int32, (8, cb), 0).astype(F32)
    octs = 8.0 * lax.broadcasted_iota(jnp.int32, (tiles, cb), 0).astype(F32)

    def weight_of(rate, residue):
        x = 2.0 * rate
        series = 1.0 - x * (1.0 / 7.0)
        for n in (6, 5, 4, 3, 2):
            series = 1.0 - (x * (1.0 / n)) * series
        return residue * jnp.sqrt(x * series)

    def columns(blk):
        return pl.ds(pl.multiple_of(blk * cb, cb), cb)

    def states(blk, _):
        at = columns(blk)
        rate = rate_ref[:, at]
        weight = weight_of(rate, res_ref[:, at])
        ww[:, at] = weight
        for n in range(modes):
            slow = jnp.exp(-rate[n : n + 1] * octs)
            eb[n] = slow
        fine = [jnp.exp(-rate[n : n + 1] * eight) for n in range(modes)]
        scaled = [fine[n] * weight[n : n + 1] for n in range(modes)]
        sums = [jnp.zeros((8, cb), F32) for _ in range(modes)]
        for t in range(tiles):
            g = grad[8 * t : 8 * t + 8, at]
            tap = jnp.zeros((8, cb), F32)
            for n in range(modes):
                level = jnp.broadcast_to(eb[n, t : t + 1], (8, cb))
                sums[n] = sums[n] + level * g
                tap = tap + level * scaled[n]
            taps[8 * t : 8 * t + 8, at] = tap
        for n in range(modes):
            rate_rows[n * nblk + blk] = rate[n : n + 1]
            u_own[n * nblk + blk] = jnp.sum(sums[n] * fine[n], axis=0, keepdims=True)
        return 0

    lax.fori_loop(0, nblk, states, 0)

    send_to_ctx(u_own, u_all, send_u, recv_u)

    for n, dy in enumerate(even):
        wait_chip(s1, r1, send1, recv1.at[n]).wait_recv()
        block = r1[:, pl.ds(y_at(dy), 1)].reshape(qs * 2 * zs, sd)
        s2[pl.ds(y_at(dy) * zs, zs)] = dot(moves[0], block).astype(BF16).reshape(zs, qs * 2, sd)
        to_plane(s2, r2, dy, send2, recv2.at[y_me])
    own = pl.ds(y_me * zs + z, 1)
    r2[own] = s2[own]

    loads[10].wait()
    loads[11].wait()
    wide = min(cols, 256)

    def inside(blk, _):
        at = pl.ds(pl.multiple_of(blk * wide, wide), wide)
        g = g_ref[:, at]
        g_spec = dot(near_in[:, : 2 * sd], jnp.concatenate([g, g], axis=0))
        high, low = split(taps[:, at])
        h_spec = dot(near_in[...], jnp.concatenate([high, high, low], axis=0))
        g_re, g_im = g_spec[:sd], g_spec[sd:]
        h_re, h_im = h_spec[:sd], h_spec[sd:]
        term = jnp.concatenate([h_re * g_re + h_im * g_im, h_re * g_im - h_im * g_re], axis=0)
        high, low = split(term)
        part = dot(near_out[...], jnp.concatenate([high, low, high], axis=0)) * (1.0 / sd)
        y[:, at] = part + gain_ref[:, at] * grad[:, at]
        return 0

    lax.fori_loop(0, cols // wide, inside, 0)

    for n, dy in enumerate(reversed(odd)):
        wait_plane(s3, r3, zs, send3, recv3.at[y_at(dy)]).wait_recv()
        block = r3[pl.ds(y_at(dy) * zs, zs)].reshape(zs * qs * 2, sd)
        s4[:, pl.ds(y_at(dy), 1)] = dot(moves[3], block).astype(BF16).reshape(qs, 1, 2 * zs, sd)
        to_chip(s4, r4, y_at(dy), send4, recv4.at[n])

    wait_ctx(u_own, u_all, send_u, recv_u).wait_recv()
    decay = jnp.exp(-rate_rows[me] * float(sd))
    state = jnp.zeros((1, cb), F32)
    for p in range(nc - 1, -1, -1):
        st_own[p] = state
        state = u_all[p] + decay * state
    send_to_ctx(st_own, st_all, send_s, recv_s)

    for n in (6, 7, 8, 9):
        loads[n].wait()
    turn_c, turn_s = twist[0], twist[1]

    def transform(part_of_y):
        half = xs * nc
        for share in range(xs):
            for arr in range(2):
                part = [blocks[a * yls + part_of_y, share * 2 + arr] for a in range(yhs)]
                freq = dot(first[...], jnp.concatenate(part + part, axis=0))
                re, im = freq[:nc], freq[nc:]
                high_re, low_re = split(re * turn_c + im * turn_s)
                high_im, low_im = split(im * turn_c - re * turn_s)
                to = pl.ds(arr * half + share * nc, nc)
                for n, piece in enumerate((high_re, high_im, low_re, low_im)):
                    left[to, n * sd : (n + 1) * sd] = piece
        both = dot(left[...], second[: 4 * sd]) + dot(left[:, : 2 * sd], second[4 * sd :])
        x_re, x_im = both[:half, :sd], both[:half, sd:]
        g_re, g_im = both[half:, :sd], both[half:, sd:]
        re = x_re * g_re + x_im * g_im
        im = x_re * g_im - x_im * g_re
        total_re = sum(re[n * nc : (n + 1) * nc] for n in range(xs))
        total_im = sum(im[n * nc : (n + 1) * nc] for n in range(xs))
        return total_re, total_im

    for n, dy in enumerate(reversed(odd)):
        wait_chip(s4, r4, send4, recv4.at[n]).wait_recv()
        block = r4[:, pl.ds(y_at(dy), 1)].reshape(qs * 2 * zs, sd)
        blocks[pl.ds(y_at(dy), 1)] = dot(moves[4], block).astype(BF16).reshape(1, xs * 2, run, sd)
    for d in range(1, yls):
        spec[:, :sd], spec[:, sd:] = transform(lax.rem(yl + d, yls))
    for dy in reversed(even):
        wait_plane(s2, r2, zs if dy else zs - 1, send2, recv2.at[y_at(dy)]).wait_recv()
        block = r2[pl.ds(y_at(dy) * zs, zs)].reshape(zs * qs * 2, sd)
        blocks[pl.ds(y_at(dy), 1)] = dot(moves[1], block).astype(BF16).reshape(1, xs * 2, run, sd)
    spec_re, spec_im = transform(yl)
    spec_re, spec_im = spec_re + spec[:, :sd], spec_im + spec[:, sd:]

    re_h, re_l = split(spec_re)
    im_h, im_l = split(-spec_im)
    both = dot(jnp.concatenate([re_h, im_h, re_l, im_l, re_h, im_h], axis=1), second[...])
    re, im = both[:, :sd], -both[:, sd:]
    high, low = split(
        jnp.concatenate([re * turn_c - im * turn_s, im * turn_c + re * turn_s], axis=0)
    )
    scale = 2.0 / (2 * nc * sd) / math.sqrt(nc * sd * nh)
    result = dot(last[...], jnp.concatenate([high, low, high], axis=0)) * scale
    for d in range(nc):
        t_own[d] = result[d : d + 1]
    send_to_ctx(t_own, t_all, send_t, recv_t)

    wait_ctx(st_own, st_all, send_s, recv_s).wait_recv()

    def outside(blk, _):
        at = columns(blk)
        rate = rate_ref[:, at]
        weight = ww[:, at]
        fine = []
        for n in range(modes):
            carried = weight[n : n + 1] * st_all[n * nblk + blk]
            eb[n] = carried * jnp.exp(-rate[n : n + 1] * (float(sd - 8) - octs))
            fine.append(jnp.exp(-rate[n : n + 1] * (8.0 - eight)))
        for t in range(tiles):
            total = y[8 * t : 8 * t + 8, at]
            for n in range(modes):
                total = total + jnp.broadcast_to(eb[n, t : t + 1], (8, cb)) * fine[n]
            y[8 * t : 8 * t + 8, at] = total
        return 0

    lax.fori_loop(0, nblk, outside, 0)

    leave = pltpu.make_async_copy(y, y_ref, y_sem)
    leave.start()

    wait_ctx(t_own, t_all, send_t, recv_t).wait_recv()
    gathered = jnp.concatenate([t_all[d] for d in range(nc)], axis=0)
    out_ref[...] = gathered

    leave.wait()
    for source, target, send in ((s1, r1, send1), (s4, r4, send4)):
        some = (pl.ds(0, qs - 1), pl.ds(0, len(even)))
        copy(some_chip, source.at[some], target.at[some], send, recv1.at[0]).wait_send()
    wait_plane(s2, r2, len(even) * zs - 1, send2, recv2.at[0]).wait_send()
    wait_plane(s3, r3, len(odd) * zs, send3, recv3.at[0]).wait_send()
    wait_ctx(u_own, u_all, send_u, recv_u).wait_send()
    wait_ctx(st_own, st_all, send_s, recv_s).wait_send()
    wait_ctx(t_own, t_all, send_t, recv_t).wait_send()


def finish(input_in, filter_in, input_out, filter_out, input_mid, filter_mid, sems):
    rows = input_in.shape[0] // 4
    pieces = [pl.ds(n * rows, rows) for n in range(4)]
    steps = [(input_in.at[p], input_mid.at[p], input_out.at[p]) for p in pieces] + [(filter_in, filter_mid, filter_out)]
    loads = [pltpu.make_async_copy(a, b, sems.at[n]) for n, (a, b, _) in enumerate(steps)]
    stores = [pltpu.make_async_copy(b, c, sems.at[len(steps) + n]) for n, (_, b, c) in enumerate(steps)]
    for load in loads:
        load.start()
    for load, store in zip(loads, stores):
        load.wait()
        store.start()
    for store in stores:
        store.wait()


def body(nc, nh, inputs, out_grad, decay_rate, residue, skip_gain):
    sd, cols = inputs.shape
    modes = decay_rate.shape[0]
    cb = modes * cols // nc
    args = (inputs, out_grad, decay_rate, residue, skip_gain.reshape(1, cols))
    args += tuple(jnp.asarray(t) for t in tables(nc, nh, sd))
    yhs, zs, cores, yls, xs = shape_of(nc, nh)
    ys, qs = yhs * yls, cores * xs
    vmem = pl.BlockSpec(memory_space=pltpu.VMEM)
    dma = pltpu.SemaphoreType.DMA
    input_grad, filter_grad = pl.pallas_call(
        functools.partial(kernel, nc, nh, modes),
        out_shape=(
            jax.ShapeDtypeStruct((sd, cols), F32),
            jax.ShapeDtypeStruct((nc, sd), F32),
        ),
        in_specs=[pl.BlockSpec(memory_space=pltpu.HBM)] * len(args),
        out_specs=(pl.BlockSpec(memory_space=pltpu.HBM), vmem),
        scratch_shapes=[pltpu.VMEM(arg.shape, arg.dtype) for arg in args]
        + [
            pltpu.VMEM((2, cols // (zs * cores), zs * cores, sd), BF16),
            pltpu.VMEM((qs, ys, 2 * zs, sd), BF16),
            pltpu.VMEM((qs, ys, 2 * zs, sd), BF16),
            pltpu.VMEM((ys * zs, qs * 2, sd), BF16),
            pltpu.VMEM((ys * zs, qs * 2, sd), BF16),
            pltpu.VMEM((ys * zs, qs * 2, sd), BF16),
            pltpu.VMEM((ys * zs, qs * 2, sd), BF16),
            pltpu.VMEM((qs, ys, 2 * zs, sd), BF16),
            pltpu.VMEM((qs, ys, 2 * zs, sd), BF16),
            pltpu.VMEM((nc, 1, cb), F32),
            pltpu.VMEM((nc, 1, cb), F32),
            pltpu.VMEM((nc, 1, cb), F32),
            pltpu.VMEM((nc, 1, cb), F32),
            pltpu.VMEM((nc, 1, sd), F32),
            pltpu.VMEM((nc, 1, sd), F32),
            pltpu.VMEM((sd, cols), F32),
            pltpu.VMEM((sd, cols), F32),
            pltpu.VMEM((sd, cols), F32),
            pltpu.VMEM((modes, sd // 8, cb), F32),
            pltpu.VMEM((modes, cols), F32),
            pltpu.VMEM((nc, 1, cb), F32),
            pltpu.VMEM((ys, xs * 2, zs * cores, sd), BF16),
            pltpu.VMEM((2 * xs * nc, 4 * sd), BF16),
            pltpu.VMEM((nc, 2 * sd), F32),
            dma((len(args),)),
            dma((ys,)),
            dma((ys,)),
            dma((ys,)),
            dma((ys,)),
        ]
        + [dma] * 11,
        compiler_params=pltpu.CompilerParams(
            collective_id=0, has_side_effects=True, vmem_limit_bytes=64 * 1024 * 1024
        ),
        name="modal_backward",
    )(*args)
    input_grad, filter_grad = pl.pallas_call(
        finish,
        out_shape=(jax.ShapeDtypeStruct((sd, cols), F32), jax.ShapeDtypeStruct((nc, sd), F32)),
        in_specs=[pl.BlockSpec(memory_space=pltpu.HBM)] * 2,
        out_specs=(pl.BlockSpec(memory_space=pltpu.HBM),) * 2,
        scratch_shapes=[pltpu.VMEM((sd, cols), F32), pltpu.VMEM((nc, sd), F32), dma((10,))],
        compiler_params=pltpu.CompilerParams(vmem_limit_bytes=64 * 1024 * 1024),
        name="finish",
    )(input_grad, filter_grad)
    return input_grad, filter_grad.T


def solution(mesh):
    placed = (P("ctx", "ch"), P("ctx", "ch"), P(), P(), P("ch"))
    return jax.shard_map(
        functools.partial(body, mesh.shape["ctx"], mesh.shape["ch"]),
        mesh=mesh,
        in_specs=placed,
        out_specs=(P("ctx", "ch"), P("ctx", "ch")),
        check_vma=False,
    )
```
